128 devices in a mesh: dp: 4 (over x), seq: 16 (over y, z_lo, core), tensor: 2 (over z_hi).
Axes of the slice: x: 4, y: 4, z: 4 (z_hi: 2, z_lo: 2; z = z_hi * 2 + z_lo), core: 2. Of those that a mesh axis runs over, the one named last changes fastest.
Arguments:
- enc_input: bfloat16 [16384, 1408], P(('dp', 'seq')), may hold values from -6 to 6
- norm_gain: float32 [1408], replicated, may hold values from 0.1 to 1.9
- fc_in: bfloat16 [1408, 6144], P(None, 'tensor'), may hold values from -0.15625 to 0.15625
- fc_out: bfloat16 [6144, 1408], P('tensor'), may hold values from -0.125 to 0.125
- final_gain: float32 [1408], replicated, may hold values from 0.1 to 1.9
- hidden_states: bfloat16 [16384, 3072], P(('dp', 'seq')), may hold values from -16 to 16
- timestep: int32 [4], P('dp'), may hold values from 0 to 999
- patch_order: int32 [256], replicated, may hold values from 0 to 255, each once
- proj_in: bfloat16 [3072, 2048], P('seq', 'tensor'), may hold values from -0.109375 to 0.109375
- proj_out: bfloat16 [1408, 2048], P('seq', 'tensor'), may hold values from -0.1875 to 0.1875
Outputs:
- state_grad: float32 [16384, 3072], P(('dp', 'seq'))
- in_grad: float32 [3072, 2048], P(('dp', 'seq'), 'tensor')
- out_grad: float32 [1408, 2048], P(('dp', 'seq'), 'tensor')
The draws below stay inside these ranges and needn't reach their ends.
Inputs may be any that keep to these rules, and one draw needn't show every extreme that they name: `patch_order`: each of the 256 positions appears once.
All inputs are finite; a program needn't handle non-finite values.
Results may differ from the reference program's by a relative error of at most 0.02.
Values may be sent and summed in bfloat16 or wider, within the bound.
A program may use at most 128 MiB of HBM per device.

```python
import jax
import jax.numpy as jnp
from jax import lax

ENC = 1408
MLP = 6144
HID = 3072
HIDP = 2048
PATCH = 256
TSTEPS = 1000
SLOTS = 16
CLIPS = 4
TOKENS = 16384
N_DP = 4
N_SEQ = 16


def set_ends(entries, rng, low, top_value):
    spot = [jax.random.randint(jax.random.fold_in(rng, axis), (), 0, length) for axis, length in enumerate(entries.shape)]
    longest = entries.shape.index(max(entries.shape))
    beside = spot[:longest] + [(spot[longest] + 1) % entries.shape[longest]] + spot[longest + 1:]
    return entries.at[tuple(spot)].set(low).at[tuple(beside)].set(top_value)


def strengthened(entries, stream_key, source, target, parts, factor):
    owner, partner = [(jnp.arange(entries.shape[axis_at]) // (entries.shape[axis_at] // parts)).reshape([-1 if axis == axis_at else 1 for axis in range(entries.ndim)]) for axis_at in (source, target)]
    chosen = jax.random.permutation(stream_key, parts)[partner]
    strong = (owner == chosen) | (owner == (partner + parts // 2) % parts)
    return jnp.where(strong, factor * entries, entries)


def block_scale(stream_key, shape, split, least, largest):
    loudness = 1.0
    for dim, blocks in split:
        steps = jax.random.uniform(jax.random.fold_in(jax.random.fold_in(stream_key, 6), dim), (blocks,), jnp.float32, least / len(split), largest / len(split))
        loudness = loudness * jnp.repeat(jnp.exp(steps), shape[dim] // blocks).reshape((-1,) + (1,) * (len(shape) - 1 - dim))
    return loudness


def centred(rng, extent, spread, most, shards=(), kind=jnp.bfloat16):
    array = jax.random.normal(rng, extent, jnp.float32) * spread
    if len(shards) > 0:
        array = block_scale(rng, extent, shards, -0.22, 0.18) * array
    return jnp.clip(array, min=-most, max=most).astype(kind)


def heavy_noise(key, extent, spread, bound, split, heavy, kind=jnp.bfloat16):
    entries = spread * jax.random.normal(key, extent, jnp.float32)
    if split:
        entries = entries * block_scale(key, extent, split, -0.22, 0.18)
    return jnp.clip(strengthened(entries, jax.random.fold_in(key, 3), *heavy), -bound, bound).astype(kind)


def setup_inputs(seed: int = 0) -> dict:
    splits = jax.random.split(jax.random.key(seed), 11)
    enc_input = centred(splits[0], (TOKENS, ENC), 1.0, 6.0, ((0, 64),))
    norm_gain = jnp.clip(1.0 + 0.18 * jax.random.normal(splits[1], (ENC,), jnp.float32), 0.1, 1.9)
    fc_in = centred(splits[2], (ENC, MLP), ENC ** -0.5, 0.15625, ((1, 2),))
    fc_out = centred(splits[3], (MLP, ENC), (MLP // 3) ** -0.5, 0.125, ((0, 2),))
    final_gain = jnp.clip(1.0 + 0.18 * jax.random.normal(splits[4], (ENC,), jnp.float32), 0.1, 1.9)
    hidden_states = heavy_noise(splits[5], (TOKENS, HID), 1.0, 16.0, ((0, 64),), (0, 1, 64, 4.0))
    timestep = set_ends(jax.random.randint(splits[6], (CLIPS,), 0, TSTEPS), jax.random.fold_in(splits[6], 1), 0, TSTEPS - 1).astype(jnp.int32)
    patch_order = jax.random.permutation(splits[7], PATCH).astype(jnp.int32)
    proj_in = centred(splits[8], (HID, HIDP), HID ** -0.5, 0.109375, ((0, 16), (1, 2)))
    proj_out = centred(splits[9], (ENC, HIDP), (HIDP // 2) ** -0.5, 0.1875, ((0, 16), (1, 2)))
    return dict(enc_input=enc_input, norm_gain=norm_gain, fc_in=fc_in, fc_out=fc_out, final_gain=final_gain, hidden_states=hidden_states, timestep=timestep, patch_order=patch_order, proj_in=proj_in, proj_out=proj_out)


def layer_norm(values, gain):
    center = lax.optimization_barrier(jnp.mean(values, axis=1, keepdims=True))
    square = lax.optimization_barrier(jnp.mean(values * values, axis=1, keepdims=True))
    return (values - center) * jax.lax.rsqrt(square - center * center + 1e-06) * gain

def reference(enc_input, norm_gain, fc_in, fc_out, final_gain, hidden_states, timestep, patch_order, proj_in, proj_out):
    inputs = enc_input.astype(jnp.float32)
    normed = layer_norm(inputs, norm_gain).astype(jnp.bfloat16)
    act = jax.nn.gelu(jnp.dot(normed, fc_in, preferred_element_type=jnp.float32), approximate=False).astype(jnp.bfloat16)
    resid = inputs + jnp.dot(act, fc_out, preferred_element_type=jnp.float32)
    feats = layer_norm(resid, final_gain).astype(jnp.bfloat16)
    share = PATCH // N_SEQ
    grid = feats.reshape(N_DP, SLOTS, PATCH, ENC)
    picked = jnp.take(grid, patch_order, axis=2).reshape(N_DP, SLOTS, N_SEQ, share, ENC)
    target = jnp.transpose(picked, (0, 2, 1, 3, 4)).reshape(TOKENS, ENC).astype(jnp.float32)
    pre = jnp.dot(hidden_states, proj_in, preferred_element_type=jnp.float32)
    pact = jax.nn.silu(pre).astype(jnp.bfloat16)
    pred = jnp.dot(pact, proj_out.T, preferred_element_type=jnp.float32)
    inv_pred = jax.lax.rsqrt(lax.optimization_barrier(jnp.sum(pred * pred, axis=1, keepdims=True)) + 1e-06)
    inv_target = jax.lax.rsqrt(lax.optimization_barrier(jnp.sum(target * target, axis=1, keepdims=True)) + 1e-06)
    cosine = lax.optimization_barrier(jnp.sum(pred * target, axis=1, keepdims=True)) * inv_pred * inv_target
    weight = (0.5 + timestep.astype(jnp.float32) / TSTEPS) * ENC
    weight = jnp.repeat(weight, TOKENS // N_DP)[:, None]
    dpred = (-weight * (inv_target * inv_pred * target - cosine * inv_pred * inv_pred * pred)).astype(jnp.bfloat16)
    dact = jnp.dot(dpred, proj_out, preferred_element_type=jnp.float32)
    sigma = jax.nn.sigmoid(pre)
    dpre = (dact * sigma * (1.0 + pre * (1.0 - sigma))).astype(jnp.bfloat16)
    state_grad = jnp.dot(dpre, proj_in.T, preferred_element_type=jnp.float32)
    factor = 1.0 / jnp.sqrt(jnp.float32(TOKENS))
    in_grad = jnp.dot(hidden_states.T, dpre, preferred_element_type=jnp.float32) * factor
    out_grad = jnp.dot(dpred.T, pact, preferred_element_type=jnp.float32) * factor
    return (state_grad, in_grad, out_grad)
```

```python
import functools
import math

import jax
import jax.numpy as jnp
from jax import lax
from jax.experimental import pallas as pl
from jax.experimental.pallas import tpu as pltpu
from jax.sharding import PartitionSpec as P

TSTEPS = 1000
MESH = pl.DeviceIdType.MESH
F32 = jnp.float32
BF16 = jnp.bfloat16
ENC = 1408
HID = 3072
CH = 512
NCH = 6
SLOTS_FC = 3


def dot(a, b):
    return jnp.dot(a, b, preferred_element_type=F32)


def dot_t(a, b):
    return lax.dot_general(a, b, (((1,), (1,)), ((), ())), preferred_element_type=F32)


def layer_norm(values, gain):
    center = jnp.mean(values, axis=-1, keepdims=True)
    square = jnp.mean(values * values, axis=-1, keepdims=True)
    return (values - center) * lax.rsqrt(square - center * center + 1e-06) * gain


def kernel(
    enc, order, ng, fg, wgt, wi, wo, hid, fcin, fcout,
    zs_out, zr_out, in_out, out_out,
    fin_b, fout_b, x_s, normed, acc, fsend, frecv, feats, target,
    win, wob, wout, hid_all, hid_t,
    pre, pact, ps, pr, predo, pzs, pzr, dp_all, dp_t, dpre,
    og, gbuf, r1, s2, r2, fin, zls, zlr, cs, cr, ss_b, sr_b, zbuf,
    fsem, lsem, asem_s, asem_r, bsem_s, bsem_r, xs, xr, ts_, tr_, gs, gr, hs, hr,
):
    x = lax.axis_index("dp")
    s = lax.axis_index("seq")
    t = lax.axis_index("tensor")
    y = s // 4
    zl = (s // 2) % 2
    c = s % 2
    q = s // 2

    def dev(x_, y_, zl_, c_, t_):
        return (x_, y_ * 4 + zl_ * 2 + c_, t_)

    sib = dev(x, y, zl, 1 - c, t)
    zpart = dev(x, y, zl, c, 1 - t)
    zlpart = dev(x, y, 1 - zl, c, t)

    def heavy(d):
        return dev((x + d * (1 - c)) % 4, (y + d * c) % 4, zl, c, t)

    def light(d):
        return dev((x + d * c) % 4, (y + d * (1 - c)) % 4, zl, c, t)

    hc = x * (1 - c) + y * c
    lc = y * (1 - c) + x * c

    def rcopy(src, dst, send, recv, to):
        return pltpu.make_async_remote_copy(
            src_ref=src, dst_ref=dst, send_sem=send, recv_sem=recv, device_id=to, device_id_type=MESH
        )

    sent = []

    def go(src, dst, send, recv, to):
        cp = rcopy(src, dst, send, recv, to)
        cp.start()
        sent.append(cp)

    def got(dst, send, recv):
        rcopy(dst, dst, send, recv, sib).wait_recv()

    def fc_copies(j):
        return (
            pltpu.make_async_copy(
                fcin.at[:, pl.ds(j * CH, CH)], fin_b.at[j % SLOTS_FC], fsem.at[0, j]
            ),
            pltpu.make_async_copy(
                fcout.at[pl.ds(j * CH, CH)], fout_b.at[j % SLOTS_FC], fsem.at[1, j]
            ),
        )

    for j in range(SLOTS_FC):
        for cp in fc_copies(j):
            cp.start()
    hid_own = pltpu.make_async_copy(hid, hid_all.at[c], lsem.at[0])
    hid_own.start()

    bar = pltpu.get_barrier_semaphore()
    for d in range(1, 16):
        pl.semaphore_signal(bar, inc=1, device_id=(x, (s + d) % 16, t), device_id_type=MESH)
    for d in range(1, 4):
        pl.semaphore_signal(bar, inc=1, device_id=((x + d) % 4, s, t), device_id_type=MESH)
    pl.semaphore_signal(bar, inc=1, device_id=zpart, device_id_type=MESH)
    pl.semaphore_wait(bar, 19)

    is_src = zl * 2 + c == x
    sa = 4 - 3 * c
    sb = 1 + 3 * c

    def blk(da, db):
        return ((lc + da + 4) % 4) * sa + ((hc + db + 4) % 4) * sb

    class Gather:
        def __init__(self, src, buf, rows, ssem, rsem, lsem_):
            self.src, self.buf, self.rows, self.ss, self.rs, self.ls = src, buf, rows, ssem, rsem, lsem_

        def half(self, h):
            return self.src.at[:, pl.ds(pl.multiple_of(h * 512, 512), 512)]

        def zero_copies(self):
            own = self.buf.at[blk(0, 0)]
            return (
                rcopy(self.half(1 - c), own, self.ss.at[0], self.rs.at[0], sib),
                rcopy(self.half(0), own, self.ss.at[1], self.rs.at[0], dev(x, y, 1 - zl, 0, t)),
                rcopy(self.half(1), own, self.ss.at[2], self.rs.at[0], dev(x, y, 1 - zl, 1, t)),
            )

        def local(self):
            return pltpu.make_async_copy(self.half(c), self.buf.at[blk(0, 0)], self.ls)

        def start0(self):
            @pl.when(is_src)
            def _():
                for cp in self.zero_copies():
                    cp.start()
                self.local().start()

        def wait0(self):
            @pl.when(is_src)
            def _():
                self.local().wait()

            @pl.when(jnp.logical_not(is_src))
            def _():
                got(self.buf.at[blk(0, 0)], self.ss.at[0], self.rs.at[0])

        def end0(self):
            @pl.when(is_src)
            def _():
                for cp in self.zero_copies():
                    cp.wait_send()

        def part(self, b, h):
            n = self.rows // 2
            return self.buf.at[b, pl.ds(h * n, n)]

        def ring(self, base, at, right, left):
            ref = self.buf.at

            def first():
                go(ref[at(0)], ref[at(0)], self.ss.at[base], self.rs.at[base], right)
                go(ref[at(0)], ref[at(0)], self.ss.at[base + 1], self.rs.at[base + 1], left)

            def from_left():
                got(ref[at(-1)], self.ss.at[base], self.rs.at[base])
                go(self.part(at(-1), 0), self.part(at(-1), 0), self.ss.at[base + 2], self.rs.at[base + 2], right)

            def from_right():
                got(ref[at(1)], self.ss.at[base + 1], self.rs.at[base + 1])
                go(self.part(at(1), 1), self.part(at(1), 1), self.ss.at[base + 3], self.rs.at[base + 3], left)

            def opposite():
                got(self.part(at(2), 0), self.ss.at[base + 2], self.rs.at[base + 2])
                got(self.part(at(2), 1), self.ss.at[base + 3], self.rs.at[base + 3])

            return first, from_left, from_right, opposite

        def stage_a(self):
            return self.ring(3, lambda d: blk(d, 0), light(1), light(3))

        def stage_b(self, i, da):
            return self.ring(7 + 4 * i, lambda d: blk(da, d), heavy(1), heavy(3))

    gi = Gather(wi, win, 192, asem_s, asem_r, lsem.at[1])
    go_ = Gather(wo, wob, 96, bsem_s, bsem_r, lsem.at[2])
    both = (gi, go_)
    for g in both:
        g.start0()
    go(hid, hid_all.at[c], hs.at[0], hr.at[0], sib)

    onehot = (lax.broadcasted_iota(jnp.int32, (256, 256), 1) == order[...]).astype(F32).astype(BF16)
    xin = dot(onehot, enc[...])
    x_s[...] = xin.reshape(2, 128, ENC)
    normed[...] = layer_norm(xin, ng[...]).astype(BF16)
    acc[...] = jnp.zeros_like(acc)

    def ffn(j):
        for cp in fc_copies(j):
            cp.wait()
        h = dot(normed[...], fin_b[j % SLOTS_FC])
        a = (0.5 * h * (1.0 + lax.erf(h * math.sqrt(0.5)))).astype(BF16)
        acc[...] += dot(a, fout_b[j % SLOTS_FC]).reshape(2, 128, ENC)
        if j + SLOTS_FC < NCH:
            for cp in fc_copies(j + SLOTS_FC):
                cp.start()

    das = (0, -1, 1, 2)
    st_a = [g.stage_a() for g in both]
    st_b = [[g.stage_b(i, das[i]) for i in range(4)] for g in both]
    for g in range(2):
        both[g].wait0()
        st_a[g][0]()
        st_b[g][0][0]()
    ffn(0)
    for g in range(2):
        st_a[g][1]()
        st_b[g][1][0]()
        st_a[g][2]()
        st_b[g][2][0]()
    ffn(1)
    for g in range(2):
        st_a[g][3]()
        st_b[g][3][0]()
    ffn(2)
    ffn(3)
    for g in range(2):
        st_b[g][0][1]()
        st_b[g][0][2]()
    ffn(4)
    ffn(5)
    fsend[...] = acc[1 - t].astype(BF16)
    go(fsend, frecv, hs.at[1], hr.at[1], zpart)
    for g in range(2):
        st_b[g][1][1]()
        st_b[g][1][2]()
    hid_own.wait()
    got(hid_all.at[1 - c], hs.at[0], hr.at[0])
    for p in range(2):
        for j in range(6):
            hid_t[j * 512:(j + 1) * 512, p * 256:(p + 1) * 256] = hid_all[p, :, j * 512:(j + 1) * 512].T
    for g in range(2):
        st_b[g][2][1]()
        st_b[g][2][2]()
    got(frecv, hs.at[1], hr.at[1])
    resid = x_s[t] + (acc[t] + frecv[...].astype(F32))
    feats[...] = layer_norm(resid, fg[...]).astype(BF16).reshape(8, 16, ENC)
    hi = s // 8
    for i in range(8):
        to = 2 * i + hi

        @pl.when(to == s)
        def _():
            pltpu.make_async_copy(feats.at[i], target.at[s % 8], ts_.at[i]).start()

        @pl.when(to != s)
        def _():
            rcopy(feats.at[i], target.at[s % 8], ts_.at[i], tr_.at[s % 8], (x, to, t)).start()

    for g in range(2):
        st_b[g][3][1]()
        st_b[g][3][2]()
    for g in range(2):
        for i in range(4):
            st_b[g][i][3]()

    wout[...] = jnp.concatenate([wob[i, 0:88].astype(F32) for i in range(16)], axis=0).astype(BF16)
    for p in range(2):
        for n in range(2):
            cols = slice(n * 256, n * 256 + 256)
            v = dot(hid_all[p], win[:, :, cols].reshape(HID, 256))
            a = (v * jax.nn.sigmoid(v)).astype(BF16)
            for h in range(2):
                pre[h, p, :, cols] = v[h * 128:h * 128 + 128]
                pact[h, p, :, cols] = a[h * 128:h * 128 + 128]
    v = dot_t(pact[1 - c].reshape(256, 512), wout[...]).astype(BF16).reshape(2, 128, ENC)
    ps[...] = v
    go(ps.at[1 - t], pr.at[1 - t], xs.at[0], xr.at[0], sib)
    go(ps.at[t], pr.at[t], xs.at[1], xr.at[1], sib)
    predo[...] = dot_t(pact[c].reshape(256, 512), wout[...]).reshape(2, 128, ENC)
    got(pr.at[1 - t], xs.at[0], xr.at[0])
    pzs[...] = (predo[1 - t] + pr[1 - t].astype(F32)).astype(BF16)
    go(pzs, pzr, xs.at[2], xr.at[2], zpart)
    for i in range(8):
        to = 2 * i + hi

        @pl.when(to == s)
        def _():
            pltpu.make_async_copy(feats.at[i], target.at[s % 8], ts_.at[i]).wait()

        @pl.when(to != s)
        def _():
            rcopy(feats.at[i], target.at[s % 8], ts_.at[i], tr_.at[s % 8], (x, to, t)).wait_send()

    for i in range(8):
        @pl.when(c * 8 + i != s)
        def _():
            got(target.at[i], ts_.at[i], tr_.at[i])

    tgt = target[...].reshape(128, ENC).astype(F32)
    inv_target = lax.rsqrt(jnp.sum(tgt * tgt, axis=1, keepdims=True) + 1e-06)
    got(pr.at[t], xs.at[1], xr.at[1])
    got(pzr, xs.at[2], xr.at[2])
    pred = predo[t] + pr[t].astype(F32) + pzr[...].astype(F32)
    inv_pred = lax.rsqrt(jnp.sum(pred * pred, axis=1, keepdims=True) + 1e-06)
    cosine = jnp.sum(pred * tgt, axis=1, keepdims=True) * inv_pred * inv_target
    weight = wgt[:, 0:1]
    dp_all[c, t] = (
        -weight * (inv_target * inv_pred * tgt - cosine * inv_pred * inv_pred * pred)
    ).astype(BF16)
    go(dp_all.at[c, t], dp_all.at[c, t], xs.at[3], xr.at[3], zpart)
    go(dp_all.at[c, t], dp_all.at[c, t], xs.at[4], xr.at[4], sib)

    def back(h, p):
        d = dp_all[h, p]
        dp_t[:, pl.ds(pl.multiple_of((h * 2 + p) * 128, 128), 128)] = d.T
        dact = dot(d, wout[...])
        v = pre[h, p]
        sigma = jax.nn.sigmoid(v)
        dpre[p, h] = (dact * sigma * (1.0 + v * (1.0 - sigma))).astype(BF16)

    back(c, t)
    got(dp_all.at[1 - c, t], xs.at[4], xr.at[4])
    back(1 - c, t)
    got(dp_all.at[c, 1 - t], xs.at[3], xr.at[3])
    go(dp_all.at[c, 1 - t], dp_all.at[c, 1 - t], xs.at[5], xr.at[5], sib)
    back(c, 1 - t)
    got(dp_all.at[1 - c, 1 - t], xs.at[5], xr.at[5])
    back(1 - c, 1 - t)

    def win_rows(j):
        return win[4 * j:4 * j + 4].reshape(768, 512)

    for j in range(4):
        ss_b[j] = dot_t(dpre[1 - c].reshape(256, 512), win_rows(j)).astype(BF16)
        go(ss_b.at[j], sr_b.at[j], gs.at[j], gr.at[j], sib)

    def state(j):
        v = dot_t(dpre[c].reshape(256, 512), win_rows(j))
        got(sr_b.at[j], gs.at[j], gr.at[j])
        zbuf[j] = (v + sr_b[j].astype(F32)).astype(BF16)
        go(zbuf.at[j], zr_out.at[j], gs.at[4 + j], gr.at[4 + j], zpart)
        pltpu.make_async_copy(zbuf.at[j], zs_out.at[j], lsem.at[3 + j]).start()

    og[pl.ds(1408, 8)] = jnp.zeros((8, 512), F32)
    for i in range(4):
        og[i * 352:(i + 1) * 352] = dot(dp_t[i * 352:(i + 1) * 352], pact[...].reshape(512, 512))

    def grad(dh, dl):
        h = (hc + dh) % 4
        l = (lc + dl) % 4
        gidx = (h * (1 - c) + l * c) * 4 + l * (1 - c) + h * c
        rows = hid_t[pl.ds(pl.multiple_of(gidx * 192, 192), 192)]
        gbuf[h, l, 0:192] = dot(rows, dpre[...].reshape(512, 512)).astype(BF16)
        gbuf[h, l, 192:288] = og[pl.ds(pl.multiple_of(gidx * 88, 8), 96)].astype(BF16)
        return h, l

    lorder = (2, 1, 3, 0)
    horder = (2, 1, 3)
    for e in range(4):
        for dh in horder:
            h, l = grad(dh, lorder[e])
            n = 8 + e * 3 + dh - 1
            go(gbuf.at[h, l], r1.at[dh - 1, lorder[e]], gs.at[n], gr.at[n], heavy(dh))
        state(e)
    for e in range(4):
        dl = lorder[e]
        h, l = grad(0, dl)
        total = gbuf[h, l].astype(F32)
        for dh in horder:
            n = 8 + e * 3 + dh - 1
            got(r1.at[dh - 1, dl], gs.at[n], gr.at[n])
            total += r1[dh - 1, dl].astype(F32)
        if dl:
            s2[dl - 1] = total.astype(BF16)
            go(s2.at[dl - 1], r2.at[dl - 1], gs.at[19 + dl], gr.at[19 + dl], light(dl))
        else:
            fin[...] = total
    for dl in (2, 1, 3):
        got(r2.at[dl - 1], gs.at[19 + dl], gr.at[19 + dl])
        fin[...] += r2[dl - 1].astype(F32)
    zls[0] = fin[pl.ds(pl.multiple_of((1 - zl) * 96, 96), 96)].astype(BF16)
    zls[1] = fin[192:288].astype(BF16)
    go(zls, zlr, gs.at[23], gr.at[23], zlpart)
    got(zlr, gs.at[23], gr.at[23])
    factor = 1.0 / 128.0
    in_sum = (fin[pl.ds(pl.multiple_of(zl * 96, 96), 96)] + zlr[0].astype(F32)) * factor
    out_sum = (fin[192:288] + zlr[1].astype(F32)) * factor
    first = c == 0
    cs[0:48] = jnp.where(first, in_sum[48:96], in_sum[0:48])
    cs[48:144] = out_sum
    go(cs, cr, gs.at[24], gr.at[24], sib)
    mine = pl.ds(pl.multiple_of(c * 512, 512), 512)
    other = pl.ds(pl.multiple_of((1 - c) * 512, 512), 512)
    in_out[:, mine] = jnp.where(first, in_sum[0:48], in_sum[48:96])
    out_out[:, mine] = out_sum
    got(cr, gs.at[24], gr.at[24])
    in_out[:, other] = cr[0:48]
    out_out[:, other] = cr[48:144]

    for j in range(4):
        got(zr_out.at[j], gs.at[4 + j], gr.at[4 + j])
        pltpu.make_async_copy(zbuf.at[j], zs_out.at[j], lsem.at[3 + j]).wait()
    for g in both:
        g.end0()
    for cp in sent:
        cp.wait_send()


def on_device(
    enc_input, norm_gain, fc_in, fc_out, final_gain, hidden_states, timestep, patch_order, proj_in, proj_out
):
    order = patch_order.reshape(8, 2, 16).transpose(1, 0, 2).reshape(256, 1)
    weight = (0.5 + timestep.astype(F32) / TSTEPS) * ENC
    weight = jnp.broadcast_to(weight.reshape(1, 1), (1, 128))
    wo = jnp.pad(proj_out, ((0, 8), (0, 0)))
    vm = pl.BlockSpec(memory_space=pltpu.VMEM)
    anyspace = pl.BlockSpec(memory_space=pl.ANY)
    V = pltpu.VMEM
    D = pltpu.SemaphoreType.DMA
    scratch = [
        V((SLOTS_FC, ENC, CH), BF16), V((SLOTS_FC, CH, ENC), BF16),
        V((2, 128, ENC), F32), V((256, ENC), BF16), V((2, 128, ENC), F32),
        V((128, ENC), BF16), V((128, ENC), BF16), V((8, 16, ENC), BF16), V((8, 16, ENC), BF16),
        V((16, 192, 512), BF16), V((16, 96, 512), BF16), V((ENC, 512), BF16),
        V((2, 256, HID), BF16), V((HID, 512), BF16),
        V((2, 2, 128, 512), F32), V((2, 2, 128, 512), BF16),
        V((2, 128, ENC), BF16), V((2, 128, ENC), BF16), V((2, 128, ENC), F32),
        V((128, ENC), BF16), V((128, ENC), BF16), V((2, 2, 128, ENC), BF16), V((ENC, 512), BF16),
        V((2, 2, 128, 512), BF16),
        V((1416, 512), F32), V((4, 4, 288, 512), BF16), V((3, 4, 288, 512), BF16),
        V((3, 288, 512), BF16), V((3, 288, 512), BF16), V((288, 512), F32),
        V((2, 96, 512), BF16), V((2, 96, 512), BF16), V((144, 512), F32), V((144, 512), F32),
        V((4, 256, 768), BF16), V((4, 256, 768), BF16), V((4, 256, 768), BF16),
        D((2, NCH)), D((7,)), D((23,)), D((23,)), D((23,)), D((23,)),
        D((6,)), D((6,)), D((8,)), D((8,)), D((25,)), D((25,)), D((2,)), D((2,)),
    ]
    zs, zr, in_grad, out_full = pl.pallas_call(
        kernel,
        out_shape=(
            jax.ShapeDtypeStruct((4, 256, 768), BF16),
            jax.ShapeDtypeStruct((4, 256, 768), BF16),
            jax.ShapeDtypeStruct((48, 1024), F32),
            jax.ShapeDtypeStruct((96, 1024), F32),
        ),
        in_specs=[vm] * 7 + [anyspace] * 3,
        out_specs=(anyspace, anyspace, vm, vm),
        scratch_shapes=scratch,
        compiler_params=pltpu.CompilerParams(
            collective_id=0, has_side_effects=True, vmem_limit_bytes=62 << 20
        ),
        name="fused",
    )(
        enc_input, order, norm_gain.reshape(1, ENC), final_gain.reshape(1, ENC), weight,
        proj_in, wo, hidden_states, fc_in, fc_out,
    )
    state_grad = zs.astype(F32) + zr.astype(F32)
    state_grad = state_grad.transpose(1, 0, 2).reshape(256, HID)
    quarter = lax.axis_index("seq") % 4
    out_grad = lax.dynamic_slice_in_dim(out_full, quarter * 22, 22, axis=0)
    return (state_grad, in_grad, out_grad)


def solution(mesh):
    in_specs = (
        P(("dp", "seq"), None),
        P(),
        P(None, "tensor"),
        P("tensor", None),
        P(),
        P(("dp", "seq"), None),
        P("dp"),
        P(),
        P("seq", "tensor"),
        P("seq", "tensor"),
    )
    out_specs = (P(("dp", "seq"), None), P(("dp", "seq"), "tensor"), P(("dp", "seq"), "tensor"))
    return jax.shard_map(
        on_device, mesh=mesh, in_specs=in_specs, out_specs=out_specs, check_vma=False
    )
```

```python
import functools
import math

import jax
import jax.numpy as jnp
from jax import lax
from jax.experimental import pallas as pl
from jax.experimental.pallas import tpu as pltpu
from jax.sharding import PartitionSpec as P

TSTEPS = 1000
MESH = pl.DeviceIdType.MESH
F32 = jnp.float32
BF16 = jnp.bfloat16
ENC = 1408
HID = 3072
CH = 512
NCH = 6
SLOTS_FC = 3


def dot(a, b):
    return jnp.dot(a, b, preferred_element_type=F32)


def dot_t(a, b):
    return lax.dot_general(a, b, (((1,), (1,)), ((), ())), preferred_element_type=F32)


def layer_norm(values, gain):
    center = jnp.mean(values, axis=-1, keepdims=True)
    square = jnp.mean(values * values, axis=-1, keepdims=True)
    return (values - center) * lax.rsqrt(square - center * center + 1e-06) * gain


def kernel(
    enc, order, ng, fg, steps, wi, wo_raw, hid, fcin, fcout,
    zs_out, zr_out, in_out, out_out,
    wo, fin_b, fout_b, x_s, normed, acc, fsend, frecv, feats, target,
    win, wob, wout, hid_all, hid_t,
    pre, pact, ps, pr, predo, pzs, pzr, dp_all, dp_t, dpre,
    og, gbuf, r1, s2, r2, fin, zls, zlr, cs, cr, ss_b, sr_b, zbuf,
    fsem, lsem, asem_s, asem_r, bsem_s, bsem_r, xs, xr, ts_, tr_, gs, gr, hs, hr,
):
    x = lax.axis_index("dp")
    s = lax.axis_index("seq")
    t = lax.axis_index("tensor")
    y = s // 4
    zl = (s // 2) % 2
    c = s % 2
    q = s // 2

    def dev(x_, y_, zl_, c_, t_):
        return (x_, y_ * 4 + zl_ * 2 + c_, t_)

    sib = dev(x, y, zl, 1 - c, t)
    zpart = dev(x, y, zl, c, 1 - t)
    zlpart = dev(x, y, 1 - zl, c, t)

    def heavy(d):
        return dev((x + d * (1 - c)) % 4, (y + d * c) % 4, zl, c, t)

    def light(d):
        return dev((x + d * c) % 4, (y + d * (1 - c)) % 4, zl, c, t)

    hc = x * (1 - c) + y * c
    lc = y * (1 - c) + x * c

    def rcopy(src, dst, send, recv, to):
        return pltpu.make_async_remote_copy(
            src_ref=src, dst_ref=dst, send_sem=send, recv_sem=recv, device_id=to, device_id_type=MESH
        )

    sent = []

    def go(src, dst, send, recv, to):
        cp = rcopy(src, dst, send, recv, to)
        cp.start()
        sent.append(cp)

    def got(dst, send, recv):
        rcopy(dst, dst, send, recv, sib).wait_recv()

    def fc_copies(j):
        return (
            pltpu.make_async_copy(
                fcin.at[:, pl.ds(j * CH, CH)], fin_b.at[j % SLOTS_FC], fsem.at[0, j]
            ),
            pltpu.make_async_copy(
                fcout.at[pl.ds(j * CH, CH)], fout_b.at[j % SLOTS_FC], fsem.at[1, j]
            ),
        )

    for j in range(SLOTS_FC):
        for cp in fc_copies(j):
            cp.start()
    hid_own = pltpu.make_async_copy(hid, hid_all.at[c], lsem.at[0])
    hid_own.start()

    wo[0:88] = wo_raw[...]
    wo[88:96] = jnp.zeros((8, 1024), BF16)

    bar = pltpu.get_barrier_semaphore()
    for d in range(1, 16):
        pl.semaphore_signal(bar, inc=1, device_id=(x, (s + d) % 16, t), device_id_type=MESH)
    for d in range(1, 4):
        pl.semaphore_signal(bar, inc=1, device_id=((x + d) % 4, s, t), device_id_type=MESH)
    pl.semaphore_signal(bar, inc=1, device_id=zpart, device_id_type=MESH)
    pl.semaphore_wait(bar, 19)

    is_src = zl * 2 + c == x
    sa = 4 - 3 * c
    sb = 1 + 3 * c

    def blk(da, db):
        return ((lc + da + 4) % 4) * sa + ((hc + db + 4) % 4) * sb

    class Gather:
        def __init__(self, src, buf, rows, ssem, rsem, lsem_):
            self.src, self.buf, self.rows, self.ss, self.rs, self.ls = src, buf, rows, ssem, rsem, lsem_

        def half(self, h):
            return self.src.at[:, pl.ds(pl.multiple_of(h * 512, 512), 512)]

        def zero_copies(self):
            own = self.buf.at[blk(0, 0)]
            return (
                rcopy(self.half(1 - c), own, self.ss.at[0], self.rs.at[0], sib),
                rcopy(self.half(0), own, self.ss.at[1], self.rs.at[0], dev(x, y, 1 - zl, 0, t)),
                rcopy(self.half(1), own, self.ss.at[2], self.rs.at[0], dev(x, y, 1 - zl, 1, t)),
            )

        def local(self):
            return pltpu.make_async_copy(self.half(c), self.buf.at[blk(0, 0)], self.ls)

        def start0(self):
            @pl.when(is_src)
            def _():
                for cp in self.zero_copies():
                    cp.start()
                self.local().start()

        def wait0(self):
            @pl.when(is_src)
            def _():
                self.local().wait()

            @pl.when(jnp.logical_not(is_src))
            def _():
                got(self.buf.at[blk(0, 0)], self.ss.at[0], self.rs.at[0])

        def end0(self):
            @pl.when(is_src)
            def _():
                for cp in self.zero_copies():
                    cp.wait_send()

        def part(self, b, h):
            n = self.rows // 2
            return self.buf.at[b, pl.ds(h * n, n)]

        def ring(self, base, at, right, left):
            ref = self.buf.at

            def first():
                go(ref[at(0)], ref[at(0)], self.ss.at[base], self.rs.at[base], right)
                go(ref[at(0)], ref[at(0)], self.ss.at[base + 1], self.rs.at[base + 1], left)

            def from_left():
                got(ref[at(-1)], self.ss.at[base], self.rs.at[base])
                go(self.part(at(-1), 0), self.part(at(-1), 0), self.ss.at[base + 2], self.rs.at[base + 2], right)

            def from_right():
                got(ref[at(1)], self.ss.at[base + 1], self.rs.at[base + 1])
                go(self.part(at(1), 1), self.part(at(1), 1), self.ss.at[base + 3], self.rs.at[base + 3], left)

            def opposite():
                got(self.part(at(2), 0), self.ss.at[base + 2], self.rs.at[base + 2])
                got(self.part(at(2), 1), self.ss.at[base + 3], self.rs.at[base + 3])

            return first, from_left, from_right, opposite

        def stage_a(self):
            return self.ring(3, lambda d: blk(d, 0), light(1), light(3))

        def stage_b(self, i, da):
            return self.ring(7 + 4 * i, lambda d: blk(da, d), heavy(1), heavy(3))

    gi = Gather(wi, win, 192, asem_s, asem_r, lsem.at[1])
    go_ = Gather(wo, wob, 96, bsem_s, bsem_r, lsem.at[2])
    both = (gi, go_)
    for g in both:
        g.start0()
    go(hid, hid_all.at[c], hs.at[0], hr.at[0], sib)

    onehot = (lax.broadcasted_iota(jnp.int32, (256, 256), 0) == order[...].reshape(1, 256)).astype(F32)
    xin = dot(onehot.T.astype(BF16), enc[...])
    xin = jnp.swapaxes(xin.reshape(8, 2, 16, ENC), 0, 1).reshape(256, ENC)
    x_s[...] = xin.reshape(2, 128, ENC)
    normed[...] = layer_norm(xin, ng[...].reshape(1, ENC)).astype(BF16)
    acc[...] = jnp.zeros_like(acc)

    def ffn(j):
        for cp in fc_copies(j):
            cp.wait()
        h = dot(normed[...], fin_b[j % SLOTS_FC])
        a = (0.5 * h * (1.0 + lax.erf(h * math.sqrt(0.5)))).astype(BF16)
        acc[...] += dot(a, fout_b[j % SLOTS_FC]).reshape(2, 128, ENC)
        if j + SLOTS_FC < NCH:
            for cp in fc_copies(j + SLOTS_FC):
                cp.start()

    das = (0, -1, 1, 2)
    st_a = [g.stage_a() for g in both]
    st_b = [[g.stage_b(i, das[i]) for i in range(4)] for g in both]
    for g in range(2):
        both[g].wait0()
        st_a[g][0]()
        st_b[g][0][0]()
    ffn(0)
    for g in range(2):
        st_a[g][1]()
        st_b[g][1][0]()
        st_a[g][2]()
        st_b[g][2][0]()
    ffn(1)
    for g in range(2):
        st_a[g][3]()
        st_b[g][3][0]()
    ffn(2)
    ffn(3)
    for g in range(2):
        st_b[g][0][1]()
        st_b[g][0][2]()
    ffn(4)
    ffn(5)
    fsend[...] = acc[1 - t].astype(BF16)
    go(fsend, frecv, hs.at[1], hr.at[1], zpart)
    for g in range(2):
        st_b[g][1][1]()
        st_b[g][1][2]()
    hid_own.wait()
    got(hid_all.at[1 - c], hs.at[0], hr.at[0])
    for p in range(2):
        for j in range(6):
            hid_t[j * 512:(j + 1) * 512, p * 256:(p + 1) * 256] = hid_all[p, :, j * 512:(j + 1) * 512].T
    for g in range(2):
        st_b[g][2][1]()
        st_b[g][2][2]()
    got(frecv, hs.at[1], hr.at[1])
    resid = x_s[t] + (acc[t] + frecv[...].astype(F32))
    feats[...] = layer_norm(resid, fg[...].reshape(1, ENC)).astype(BF16).reshape(8, 16, ENC)
    hi = s // 8
    for i in range(8):
        to = 2 * i + hi

        @pl.when(to == s)
        def _():
            pltpu.make_async_copy(feats.at[i], target.at[s % 8], ts_.at[i]).start()

        @pl.when(to != s)
        def _():
            rcopy(feats.at[i], target.at[s % 8], ts_.at[i], tr_.at[s % 8], (x, to, t)).start()

    for g in range(2):
        st_b[g][3][1]()
        st_b[g][3][2]()
    for g in range(2):
        for i in range(4):
            st_b[g][i][3]()

    wout[...] = jnp.concatenate([wob[i, 0:88].astype(F32) for i in range(16)], axis=0).astype(BF16)
    for p in range(2):
        for n in range(2):
            cols = slice(n * 256, n * 256 + 256)
            v = dot(hid_all[p], win[:, :, cols].reshape(HID, 256))
            a = (v * jax.nn.sigmoid(v)).astype(BF16)
            for h in range(2):
                pre[h, p, :, cols] = v[h * 128:h * 128 + 128]
                pact[h, p, :, cols] = a[h * 128:h * 128 + 128]
    v = dot_t(pact[1 - c].reshape(256, 512), wout[...]).astype(BF16).reshape(2, 128, ENC)
    ps[...] = v
    go(ps.at[1 - t], pr.at[1 - t], xs.at[0], xr.at[0], sib)
    go(ps.at[t], pr.at[t], xs.at[1], xr.at[1], sib)
    predo[...] = dot_t(pact[c].reshape(256, 512), wout[...]).reshape(2, 128, ENC)
    got(pr.at[1 - t], xs.at[0], xr.at[0])
    pzs[...] = (predo[1 - t] + pr[1 - t].astype(F32)).astype(BF16)
    go(pzs, pzr, xs.at[2], xr.at[2], zpart)
    for i in range(8):
        to = 2 * i + hi

        @pl.when(to == s)
        def _():
            pltpu.make_async_copy(feats.at[i], target.at[s % 8], ts_.at[i]).wait()

        @pl.when(to != s)
        def _():
            rcopy(feats.at[i], target.at[s % 8], ts_.at[i], tr_.at[s % 8], (x, to, t)).wait_send()

    for i in range(8):
        @pl.when(c * 8 + i != s)
        def _():
            got(target.at[i], ts_.at[i], tr_.at[i])

    tgt = target[...].reshape(128, ENC).astype(F32)
    inv_target = lax.rsqrt(jnp.sum(tgt * tgt, axis=1, keepdims=True) + 1e-06)
    got(pr.at[t], xs.at[1], xr.at[1])
    got(pzr, xs.at[2], xr.at[2])
    pred = predo[t] + pr[t].astype(F32) + pzr[...].astype(F32)
    inv_pred = lax.rsqrt(jnp.sum(pred * pred, axis=1, keepdims=True) + 1e-06)
    cosine = jnp.sum(pred * tgt, axis=1, keepdims=True) * inv_pred * inv_target
    weight = (0.5 + steps[0].astype(F32) / TSTEPS) * ENC
    dp_all[c, t] = (
        -weight * (inv_target * inv_pred * tgt - cosine * inv_pred * inv_pred * pred)
    ).astype(BF16)
    go(dp_all.at[c, t], dp_all.at[c, t], xs.at[3], xr.at[3], zpart)
    go(dp_all.at[c, t], dp_all.at[c, t], xs.at[4], xr.at[4], sib)

    def back(h, p):
        d = dp_all[h, p]
        dp_t[:, pl.ds(pl.multiple_of((h * 2 + p) * 128, 128), 128)] = d.T
        dact = dot(d, wout[...])
        v = pre[h, p]
        sigma = jax.nn.sigmoid(v)
        dpre[p, h] = (dact * sigma * (1.0 + v * (1.0 - sigma))).astype(BF16)

    back(c, t)
    got(dp_all.at[1 - c, t], xs.at[4], xr.at[4])
    back(1 - c, t)
    got(dp_all.at[c, 1 - t], xs.at[3], xr.at[3])
    go(dp_all.at[c, 1 - t], dp_all.at[c, 1 - t], xs.at[5], xr.at[5], sib)
    back(c, 1 - t)
    got(dp_all.at[1 - c, 1 - t], xs.at[5], xr.at[5])
    back(1 - c, 1 - t)

    def win_rows(j):
        return win[4 * j:4 * j + 4].reshape(768, 512)

    for j in range(4):
        ss_b[j] = dot_t(dpre[1 - c].reshape(256, 512), win_rows(j)).astype(BF16)
        go(ss_b.at[j], sr_b.at[j], gs.at[j], gr.at[j], sib)

    def state(j):
        v = dot_t(dpre[c].reshape(256, 512), win_rows(j))
        got(sr_b.at[j], gs.at[j], gr.at[j])
        zbuf[j] = (v + sr_b[j].astype(F32)).astype(BF16)
        go(zbuf.at[j], zr_out.at[:, pl.ds(j * 768, 768)], gs.at[4 + j], gr.at[4 + j], zpart)
        pltpu.make_async_copy(zbuf.at[j], zs_out.at[:, pl.ds(j * 768, 768)], lsem.at[3 + j]).start()

    og[pl.ds(1408, 8)] = jnp.zeros((8, 512), F32)
    for i in range(4):
        og[i * 352:(i + 1) * 352] = dot(dp_t[i * 352:(i + 1) * 352], pact[...].reshape(512, 512))

    def grad(dh, dl):
        h = (hc + dh) % 4
        l = (lc + dl) % 4
        gidx = (h * (1 - c) + l * c) * 4 + l * (1 - c) + h * c
        rows = hid_t[pl.ds(pl.multiple_of(gidx * 192, 192), 192)]
        gbuf[h, l, 0:192] = dot(rows, dpre[...].reshape(512, 512)).astype(BF16)
        gbuf[h, l, 192:288] = og[pl.ds(pl.multiple_of(gidx * 88, 8), 96)].astype(BF16)
        return h, l

    lorder = (2, 1, 3, 0)
    horder = (2, 1, 3)
    for e in range(4):
        for dh in horder:
            h, l = grad(dh, lorder[e])
            n = 8 + e * 3 + dh - 1
            go(gbuf.at[h, l], r1.at[dh - 1, lorder[e]], gs.at[n], gr.at[n], heavy(dh))
        state(e)
    for e in range(4):
        dl = lorder[e]
        h, l = grad(0, dl)
        total = gbuf[h, l].astype(F32)
        for dh in horder:
            n = 8 + e * 3 + dh - 1
            got(r1.at[dh - 1, dl], gs.at[n], gr.at[n])
            total += r1[dh - 1, dl].astype(F32)
        if dl:
            s2[dl - 1] = total.astype(BF16)
            go(s2.at[dl - 1], r2.at[dl - 1], gs.at[19 + dl], gr.at[19 + dl], light(dl))
        else:
            fin[...] = total
    for dl in (2, 1, 3):
        got(r2.at[dl - 1], gs.at[19 + dl], gr.at[19 + dl])
        fin[...] += r2[dl - 1].astype(F32)
    zls[0] = fin[pl.ds(pl.multiple_of((1 - zl) * 96, 96), 96)].astype(BF16)
    zls[1] = fin[192:288].astype(BF16)
    go(zls, zlr, gs.at[23], gr.at[23], zlpart)
    got(zlr, gs.at[23], gr.at[23])
    factor = 1.0 / 128.0
    in_sum = (fin[pl.ds(pl.multiple_of(zl * 96, 96), 96)] + zlr[0].astype(F32)) * factor
    out_sum = (fin[192:288] + zlr[1].astype(F32)) * factor
    first = c == 0

    def quarter(i):
        lo = jnp.where(i % 2 == 0, out_sum[0:22], out_sum[22:44])
        hi_ = jnp.where(i % 2 == 0, out_sum[44:66], out_sum[66:88])
        return jnp.where(i < 2, lo, hi_)

    cs[0:48] = jnp.where(first, in_sum[48:96], in_sum[0:48])
    cs[48:70] = quarter(zl * 2 + 1 - c)
    cs[70:72] = jnp.zeros((2, 512), F32)
    go(cs, cr, gs.at[24], gr.at[24], sib)
    mine = pl.ds(pl.multiple_of(c * 512, 512), 512)
    other = pl.ds(pl.multiple_of((1 - c) * 512, 512), 512)
    in_out[:, mine] = jnp.where(first, in_sum[0:48], in_sum[48:96])
    out_out[:, mine] = quarter(zl * 2 + c)
    got(cr, gs.at[24], gr.at[24])
    in_out[:, other] = cr[0:48]
    out_out[:, other] = cr[48:70]

    for j in range(4):
        got(zr_out.at[:, pl.ds(j * 768, 768)], gs.at[4 + j], gr.at[4 + j])
        pltpu.make_async_copy(zbuf.at[j], zs_out.at[:, pl.ds(j * 768, 768)], lsem.at[3 + j]).wait()
    for g in both:
        g.end0()
    for cp in sent:
        cp.wait_send()


def on_device(
    enc_input, norm_gain, fc_in, fc_out, final_gain, hidden_states, timestep, patch_order, proj_in, proj_out
):
    vm = pl.BlockSpec(memory_space=pltpu.VMEM)
    anyspace = pl.BlockSpec(memory_space=pl.ANY)
    V = pltpu.VMEM
    D = pltpu.SemaphoreType.DMA
    scratch = [
        V((96, 1024), BF16), V((SLOTS_FC, ENC, CH), BF16), V((SLOTS_FC, CH, ENC), BF16),
        V((2, 128, ENC), F32), V((256, ENC), BF16), V((2, 128, ENC), F32),
        V((128, ENC), BF16), V((128, ENC), BF16), V((8, 16, ENC), BF16), V((8, 16, ENC), BF16),
        V((16, 192, 512), BF16), V((16, 96, 512), BF16), V((ENC, 512), BF16),
        V((2, 256, HID), BF16), V((HID, 512), BF16),
        V((2, 2, 128, 512), F32), V((2, 2, 128, 512), BF16),
        V((2, 128, ENC), BF16), V((2, 128, ENC), BF16), V((2, 128, ENC), F32),
        V((128, ENC), BF16), V((128, ENC), BF16), V((2, 2, 128, ENC), BF16), V((ENC, 512), BF16),
        V((2, 2, 128, 512), BF16),
        V((1416, 512), F32), V((4, 4, 288, 512), BF16), V((3, 4, 288, 512), BF16),
        V((3, 288, 512), BF16), V((3, 288, 512), BF16), V((288, 512), F32),
        V((2, 96, 512), BF16), V((2, 96, 512), BF16), V((72, 512), F32), V((72, 512), F32),
        V((4, 256, 768), BF16), V((4, 256, 768), BF16), V((4, 256, 768), BF16),
        D((2, NCH)), D((7,)), D((23,)), D((23,)), D((23,)), D((23,)),
        D((6,)), D((6,)), D((8,)), D((8,)), D((25,)), D((25,)), D((2,)), D((2,)),
    ]
    zs, zr, in_grad, out_grad = pl.pallas_call(
        kernel,
        out_shape=(
            jax.ShapeDtypeStruct((256, HID), BF16),
            jax.ShapeDtypeStruct((256, HID), BF16),
            jax.ShapeDtypeStruct((48, 1024), F32),
            jax.ShapeDtypeStruct((22, 1024), F32),
        ),
        in_specs=[vm] * 4 + [pl.BlockSpec(memory_space=pltpu.SMEM)] + [vm] * 2 + [anyspace] * 3,
        out_specs=(anyspace, anyspace, vm, vm),
        scratch_shapes=scratch,
        compiler_params=pltpu.CompilerParams(
            collective_id=0, has_side_effects=True, vmem_limit_bytes=62 << 20
        ),
        name="fused",
    )(
        enc_input, patch_order, norm_gain, final_gain, timestep,
        proj_in, proj_out, hidden_states, fc_in, fc_out,
    )
    state_grad = zs.astype(F32) + zr.astype(F32)
    return (state_grad, in_grad, out_grad)


def solution(mesh):
    in_specs = (
        P(("dp", "seq"), None),
        P(),
        P(None, "tensor"),
        P("tensor", None),
        P(),
        P(("dp", "seq"), None),
        P("dp"),
        P(),
        P("seq", "tensor"),
        P("seq", "tensor"),
    )
    out_specs = (P(("dp", "seq"), None), P(("dp", "seq"), "tensor"), P(("dp", "seq"), "tensor"))
    return jax.shard_map(
        on_device, mesh=mesh, in_specs=in_specs, out_specs=out_specs, check_vma=False
    )
```

```python
import functools
import math

import jax
import jax.numpy as jnp
from jax import lax
from jax.experimental import pallas as pl
from jax.experimental.pallas import tpu as pltpu
from jax.sharding import PartitionSpec as P

TSTEPS = 1000
MESH = pl.DeviceIdType.MESH
F32 = jnp.float32
BF16 = jnp.bfloat16
ENC = 1408
HID = 3072
CH = 512
NCH = 6
SLOTS_FC = 3


def dot(a, b):
    return jnp.dot(a, b, preferred_element_type=F32)


def dot_t(a, b):
    return lax.dot_general(a, b, (((1,), (1,)), ((), ())), preferred_element_type=F32)


def layer_norm(values, gain):
    center = jnp.mean(values, axis=-1, keepdims=True)
    square = jnp.mean(values * values, axis=-1, keepdims=True)
    return (values - center) * lax.rsqrt(square - center * center + 1e-06) * gain


def kernel(
    enc, order, ng, fg, steps, wi, wo_raw, hid, fcin, fcout,
    zs_out, zr_out, in_out, out_out,
    wo, fin_b, fout_b, x_s, normed, acc, fsend, frecv, feats, target,
    win, wob, wout, hid_all, hid_t,
    pre, pact, ps, pr, predo, pzs, pzr, dp_all, dp_t, dpre,
    og, gbuf, rh, r1, s2, r2, fin, cs, cr, ss_b, sr_b, zbuf,
    fsem, lsem, asem_s, asem_r, bsem_s, bsem_r, xs, xr, ts_, tr_, gs, gr, hs, hr,
):
    x = lax.axis_index("dp")
    s = lax.axis_index("seq")
    t = lax.axis_index("tensor")
    y = s // 4
    zl = (s // 2) % 2
    c = s % 2
    q = s // 2

    def dev(x_, y_, zl_, c_, t_):
        return (x_, y_ * 4 + zl_ * 2 + c_, t_)

    sib = dev(x, y, zl, 1 - c, t)
    zpart = dev(x, y, zl, c, 1 - t)
    zlpart = dev(x, y, 1 - zl, c, t)

    def heavy(d):
        return dev((x + d * (1 - c)) % 4, (y + d * c) % 4, zl, c, t)

    def light(d):
        return dev((x + d * c) % 4, (y + d * (1 - c)) % 4, zl, c, t)

    hc = x * (1 - c) + y * c
    lc = y * (1 - c) + x * c

    def rcopy(src, dst, send, recv, to):
        return pltpu.make_async_remote_copy(
            src_ref=src, dst_ref=dst, send_sem=send, recv_sem=recv, device_id=to, device_id_type=MESH
        )

    sent = []

    def go(src, dst, send, recv, to):
        cp = rcopy(src, dst, send, recv, to)
        cp.start()
        sent.append(cp)

    def got(dst, send, recv):
        rcopy(dst, dst, send, recv, sib).wait_recv()

    def fc_copies(j):
        return (
            pltpu.make_async_copy(
                fcin.at[:, pl.ds(j * CH, CH)], fin_b.at[j % SLOTS_FC], fsem.at[0, j]
            ),
            pltpu.make_async_copy(
                fcout.at[pl.ds(j * CH, CH)], fout_b.at[j % SLOTS_FC], fsem.at[1, j]
            ),
        )

    for j in range(SLOTS_FC):
        for cp in fc_copies(j):
            cp.start()
    hid_own = pltpu.make_async_copy(hid, hid_all.at[c], lsem.at[0])
    hid_own.start()

    wo[0:88] = wo_raw[...]
    wo[88:96] = jnp.zeros((8, 1024), BF16)

    bar = pltpu.get_barrier_semaphore()
    for d in range(1, 16):
        pl.semaphore_signal(bar, inc=1, device_id=(x, (s + d) % 16, t), device_id_type=MESH)
    for d in range(1, 4):
        pl.semaphore_signal(bar, inc=1, device_id=((x + d) % 4, s, t), device_id_type=MESH)
    pl.semaphore_signal(bar, inc=1, device_id=zpart, device_id_type=MESH)
    pl.semaphore_wait(bar, 19)

    is_src = c == x // 2

    class Gather:
        def __init__(self, src, buf, rows, ssem, rsem, lsem_):
            self.src, self.buf, self.rows, self.ss, self.rs, self.ls = src, buf, rows, ssem, rsem, lsem_

        def piece(self, da, db, z):
            yy = (y + da * (1 - c) + db * c + 4) % 4
            xx = (x + da * c + db * (1 - c) + 4) % 4
            if z == 2:
                return self.buf.at[yy, :, xx]
            return self.buf.at[yy, zl if z == 0 else 1 - zl, xx]

        def half(self, h):
            n = self.rows
            return self.src.at[pl.ds(pl.multiple_of((x % 2) * n, n), n), pl.ds(pl.multiple_of(h * 512, 512), 512)]

        def zero_copies(self):
            own = self.piece(0, 0, 0)
            return (
                rcopy(self.half(1 - c), own, self.ss.at[0], self.rs.at[0], sib),
                rcopy(self.half(0), own, self.ss.at[1], self.rs.at[1], dev(x, y, 1 - zl, 0, t)),
                rcopy(self.half(1), own, self.ss.at[2], self.rs.at[1], dev(x, y, 1 - zl, 1, t)),
            )

        def local(self):
            return pltpu.make_async_copy(self.half(c), self.piece(0, 0, 0), self.ls)

        def start0(self):
            @pl.when(is_src)
            def _():
                for cp in self.zero_copies():
                    cp.start()
                self.local().start()

        def end0(self):
            @pl.when(is_src)
            def _():
                for cp in self.zero_copies():
                    cp.wait_send()

        def put(self, n, ref, to):
            go(ref, ref, self.ss.at[n], self.rs.at[n], to)

        def take(self, n, ref):
            got(ref, self.ss.at[n], self.rs.at[n])

        def native(self):
            @pl.when(is_src)
            def _():
                self.local().wait()

            @pl.when(jnp.logical_not(is_src))
            def _():
                self.take(0, self.piece(0, 0, 0))

            self.begin(0)

        def foreign(self):
            self.take(1, self.piece(0, 0, 1))
            self.begin(1)

        def begin(self, z):
            own = self.piece(0, 0, z)
            self.put(3 + 4 * z, own, light(1))
            self.put(4 + 4 * z, own, light(3))
            self.put(5 + 4 * z, own, heavy(1))
            self.put(6 + 4 * z, own, heavy(3))

        def light_near(self):
            self.take(3, self.piece(-1, 0, 0))
            self.put(11, self.piece(-1, 0, 0), light(1))
            self.take(8, self.piece(1, 0, 1))
            self.put(12, self.piece(1, 0, 1), light(3))
            self.take(7, self.piece(-1, 0, 1))
            self.take(4, self.piece(1, 0, 0))
            for k, da in ((13, -1), (15, 1)):
                self.put(k, self.piece(da, 0, 2), heavy(1))
                self.put(k + 1, self.piece(da, 0, 2), heavy(3))

        def light_far(self):
            self.take(11, self.piece(2, 0, 0))
            self.take(12, self.piece(2, 0, 1))
            self.put(17, self.piece(2, 0, 2), heavy(1))
            self.put(18, self.piece(2, 0, 2), heavy(3))

        def heavy_own(self):
            self.take(5, self.piece(0, -1, 0))
            self.put(19, self.piece(0, -1, 0), heavy(1))
            self.take(10, self.piece(0, 1, 1))
            self.put(20, self.piece(0, 1, 1), heavy(3))

        def heavy_other(self, i):
            da = (-1, 1, 2)[i]
            self.take(13 + 2 * i, self.piece(da, -1, 2))
            self.put(21 + 2 * i, self.piece(da, -1, 0), heavy(1))
            self.take(14 + 2 * i, self.piece(da, 1, 2))
            self.put(22 + 2 * i, self.piece(da, 1, 1), heavy(3))

        def finish(self):
            self.take(9, self.piece(0, -1, 1))
            self.take(6, self.piece(0, 1, 0))
            for k, da in ((19, 0), (21, -1), (23, 1), (25, 2)):
                self.take(k, self.piece(da, 2, 0))
                self.take(k + 1, self.piece(da, 2, 1))

    gi = Gather(wi, win, 96, asem_s, asem_r, lsem.at[1])
    go_ = Gather(wo, wob, 48, bsem_s, bsem_r, lsem.at[2])
    both = (gi, go_)
    for g in both:
        g.start0()
    go(hid, hid_all.at[c], hs.at[0], hr.at[0], sib)

    onehot = (lax.broadcasted_iota(jnp.int32, (256, 256), 0) == order[...].reshape(1, 256)).astype(F32)
    xin = dot(onehot.T.astype(BF16), enc[...])
    xin = jnp.swapaxes(xin.reshape(8, 2, 16, ENC), 0, 1).reshape(256, ENC)
    x_s[...] = xin.reshape(2, 128, ENC)
    normed[...] = layer_norm(xin, ng[...].reshape(1, ENC)).astype(BF16)
    acc[...] = jnp.zeros_like(acc)

    def ffn(j):
        for cp in fc_copies(j):
            cp.wait()
        h = dot(normed[...], fin_b[j % SLOTS_FC])
        a = (0.5 * h * (1.0 + lax.erf(h * math.sqrt(0.5)))).astype(BF16)
        acc[...] += dot(a, fout_b[j % SLOTS_FC]).reshape(2, 128, ENC)
        if j + SLOTS_FC < NCH:
            for cp in fc_copies(j + SLOTS_FC):
                cp.start()

    for g in both:
        g.native()
    for g in both:
        g.foreign()
    ffn(0)
    gi.light_near()
    ffn(1)
    gi.light_far()
    go_.light_near()
    ffn(2)
    gi.heavy_own()
    go_.light_far()
    ffn(3)
    gi.heavy_other(0)
    ffn(4)
    gi.heavy_other(1)
    ffn(5)
    fsend[...] = acc[1 - t].astype(BF16)
    go(fsend, frecv, hs.at[1], hr.at[1], zpart)
    gi.heavy_other(2)
    go_.heavy_own()
    hid_own.wait()
    got(hid_all.at[1 - c], hs.at[0], hr.at[0])
    for p in range(2):
        for j in range(6):
            hid_t[j * 512:(j + 1) * 512, p * 256:(p + 1) * 256] = hid_all[p, :, j * 512:(j + 1) * 512].T
    go_.heavy_other(0)
    go_.heavy_other(1)
    gi.finish()
    go_.heavy_other(2)

    for p in range(2):
        for n in range(2):
            cols = slice(n * 256, n * 256 + 256)
            v = dot(hid_all[p], win[:, :, :, :, cols].reshape(HID, 256))
            a = (v * jax.nn.sigmoid(v)).astype(BF16)
            for h in range(2):
                pre[h, p, :, cols] = v[h * 128:h * 128 + 128]
                pact[h, p, :, cols] = a[h * 128:h * 128 + 128]
    go_.finish()
    wout[...] = jnp.concatenate(
        [wob[i, z, 2 * k:2 * k + 2].reshape(96, 512)[0:88].astype(F32) for i in range(4) for z in range(2) for k in range(2)],
        axis=0,
    ).astype(BF16)
    v = dot_t(pact[1 - c].reshape(256, 512), wout[...]).astype(BF16).reshape(2, 128, ENC)
    ps[...] = v
    go(ps.at[1 - t], pr.at[1 - t], xs.at[0], xr.at[0], sib)
    go(ps.at[t], pr.at[t], xs.at[1], xr.at[1], sib)
    predo[...] = dot_t(pact[c].reshape(256, 512), wout[...]).reshape(2, 128, ENC)
    got(frecv, hs.at[1], hr.at[1])
    resid = x_s[t] + (acc[t] + frecv[...].astype(F32))
    feats[...] = layer_norm(resid, fg[...].reshape(1, ENC)).astype(BF16).reshape(8, 16, ENC)
    hi = s // 8
    for i in range(8):
        to = 2 * i + hi

        @pl.when(to == s)
        def _():
            pltpu.make_async_copy(feats.at[i], target.at[s % 8], ts_.at[i]).start()

        @pl.when(to != s)
        def _():
            rcopy(feats.at[i], target.at[s % 8], ts_.at[i], tr_.at[s % 8], (x, to, t)).start()

    got(pr.at[1 - t], xs.at[0], xr.at[0])
    pzs[...] = (predo[1 - t] + pr[1 - t].astype(F32)).astype(BF16)
    go(pzs, pzr, xs.at[2], xr.at[2], zpart)
    for i in range(8):
        to = 2 * i + hi

        @pl.when(to == s)
        def _():
            pltpu.make_async_copy(feats.at[i], target.at[s % 8], ts_.at[i]).wait()

        @pl.when(to != s)
        def _():
            rcopy(feats.at[i], target.at[s % 8], ts_.at[i], tr_.at[s % 8], (x, to, t)).wait_send()

    for i in range(8):
        @pl.when(c * 8 + i != s)
        def _():
            got(target.at[i], ts_.at[i], tr_.at[i])

    tgt = target[...].reshape(128, ENC).astype(F32)
    inv_target = lax.rsqrt(jnp.sum(tgt * tgt, axis=1, keepdims=True) + 1e-06)
    got(pr.at[t], xs.at[1], xr.at[1])
    got(pzr, xs.at[2], xr.at[2])
    pred = predo[t] + pr[t].astype(F32) + pzr[...].astype(F32)
    inv_pred = lax.rsqrt(jnp.sum(pred * pred, axis=1, keepdims=True) + 1e-06)
    cosine = jnp.sum(pred * tgt, axis=1, keepdims=True) * inv_pred * inv_target
    weight = (0.5 + steps[0].astype(F32) / TSTEPS) * ENC
    dp_all[c, t] = (
        -weight * (inv_target * inv_pred * tgt - cosine * inv_pred * inv_pred * pred)
    ).astype(BF16)
    go(dp_all.at[c, t], dp_all.at[c, t], xs.at[3], xr.at[3], zpart)
    go(dp_all.at[c, t], dp_all.at[c, t], xs.at[4], xr.at[4], sib)

    def back(h, p):
        d = dp_all[h, p]
        dp_t[:, pl.ds(pl.multiple_of((h * 2 + p) * 128, 128), 128)] = d.T
        dact = dot(d, wout[...])
        v = pre[h, p]
        sigma = jax.nn.sigmoid(v)
        dpre[p, h] = (dact * sigma * (1.0 + v * (1.0 - sigma))).astype(BF16)

    back(c, t)
    got(dp_all.at[1 - c, t], xs.at[4], xr.at[4])
    back(1 - c, t)
    got(dp_all.at[c, 1 - t], xs.at[3], xr.at[3])
    go(dp_all.at[c, 1 - t], dp_all.at[c, 1 - t], xs.at[5], xr.at[5], sib)
    back(c, 1 - t)
    got(dp_all.at[1 - c, 1 - t], xs.at[5], xr.at[5])
    back(1 - c, 1 - t)

    def win_rows(j):
        return win[j].reshape(768, 512)

    for j in range(4):
        ss_b[j] = dot_t(dpre[1 - c].reshape(256, 512), win_rows(j)).astype(BF16)
        go(ss_b.at[j], sr_b.at[j], gs.at[j], gr.at[j], sib)

    def state(j):
        v = dot_t(dpre[c].reshape(256, 512), win_rows(j))
        got(sr_b.at[j], gs.at[j], gr.at[j])
        zbuf[j] = (v + sr_b[j].astype(F32)).astype(BF16)
        go(zbuf.at[j], zr_out.at[:, pl.ds(j * 768, 768)], gs.at[4 + j], gr.at[4 + j], zpart)
        pltpu.make_async_copy(zbuf.at[j], zs_out.at[:, pl.ds(j * 768, 768)], lsem.at[3 + j]).start()

    og[pl.ds(1408, 8)] = jnp.zeros((8, 512), F32)
    for i in range(4):
        og[i * 352:(i + 1) * 352] = dot(dp_t[i * 352:(i + 1) * 352], pact[...].reshape(512, 512))

    def grad(dh, dl):
        h = (hc + dh) % 4
        l = (lc + dl) % 4
        gidx = (h * (1 - c) + l * c) * 4 + l * (1 - c) + h * c
        rows = hid_t[pl.ds(pl.multiple_of(gidx * 192, 192), 192)]
        gbuf[h, l, 0:192] = dot(rows, dpre[...].reshape(512, 512)).astype(BF16)
        gbuf[h, l, 192:288] = og[pl.ds(pl.multiple_of(gidx * 88, 8), 96)].astype(BF16)
        return h, l

    lorder = (2, 1, 3, 0)
    for e in range(4):
        dl = lorder[e]
        h, l = grad(2, dl)
        go(gbuf.at[h, l, pl.ds(0, 144)], rh.at[0, dl], gs.at[8 + 4 * e], gr.at[8 + 4 * e], heavy(1))
        go(gbuf.at[h, l, pl.ds(144, 144)], rh.at[1, dl], gs.at[9 + 4 * e], gr.at[9 + 4 * e], heavy(3))
    for e in range(4):
        dl = lorder[e]
        state(e)
        for k, dh in ((0, 1), (1, 3)):
            h, l = grad(dh, dl)
            part = pl.ds(k * 144, 144)
            n = 8 + 4 * e + k
            got(rh.at[k, dl], gs.at[n], gr.at[n])
            gbuf[h, l, part] = (gbuf[h, l, part].astype(F32) + rh[k, dl].astype(F32)).astype(BF16)
            go(gbuf.at[h, l], r1.at[k, dl], gs.at[n + 2], gr.at[n + 2], heavy(dh))
    for e in range(4):
        dl = lorder[e]
        h, l = grad(0, dl)
        total = gbuf[h, l].astype(F32)
        for k in range(2):
            n = 10 + 4 * e + k
            got(r1.at[k, dl], gs.at[n], gr.at[n])
            total += r1[k, dl].astype(F32)
        if dl:
            s2[dl - 1] = total.astype(BF16)
            go(s2.at[dl - 1], r2.at[dl - 1], gs.at[23 + dl], gr.at[23 + dl], light(dl))
        else:
            fin[...] = total
    for dl in (2, 1, 3):
        got(r2.at[dl - 1], gs.at[23 + dl], gr.at[23 + dl])
        fin[...] += r2[dl - 1].astype(F32)

    def rows_for(zl_, c_):
        even = c_ == 0
        lo = jnp.where(even, fin[192:214], fin[214:236])
        hi_ = jnp.where(even, fin[236:258], fin[258:280])
        return fin[pl.ds(pl.multiple_of(zl_ * 96 + c_ * 48, 48), 48)], jnp.where(zl_ == 0, lo, hi_)

    dests = ((1 - zl, 1 - c), (1 - zl, c), (zl, 1 - c))
    for k in range(3):
        a, b = rows_for(*dests[k])
        cs[k, 0:48] = a.astype(BF16)
        cs[k, 48:80] = jnp.concatenate([b, jnp.zeros((10, 512), F32)], axis=0).astype(BF16)
        go(cs.at[k], cr.at[k], gs.at[27 + k], gr.at[27 + k], dev(x, y, dests[k][0], dests[k][1], t))
    factor = 1.0 / 128.0
    mine = pl.ds(pl.multiple_of(c * 512, 512), 512)
    other = pl.ds(pl.multiple_of((1 - c) * 512, 512), 512)
    a, b = rows_for(zl, c)
    for k in range(3):
        got(cr.at[k], gs.at[27 + k], gr.at[27 + k])
    in_out[:, mine] = (a + cr[1, 0:48].astype(F32)) * factor
    out_out[:, mine] = (b + cr[1, 48:80].astype(F32)[0:22]) * factor
    in_out[:, other] = (cr[0, 0:48].astype(F32) + cr[2, 0:48].astype(F32)) * factor
    out_out[:, other] = (cr[0, 48:80].astype(F32) + cr[2, 48:80].astype(F32))[0:22] * factor

    for j in range(4):
        got(zr_out.at[:, pl.ds(j * 768, 768)], gs.at[4 + j], gr.at[4 + j])
        pltpu.make_async_copy(zbuf.at[j], zs_out.at[:, pl.ds(j * 768, 768)], lsem.at[3 + j]).wait()
    for g in both:
        g.end0()
    for cp in sent:
        cp.wait_send()


def on_device(
    enc_input, norm_gain, fc_in, fc_out, final_gain, hidden_states, timestep, patch_order, proj_in, proj_out
):
    vm = pl.BlockSpec(memory_space=pltpu.VMEM)
    anyspace = pl.BlockSpec(memory_space=pl.ANY)
    V = pltpu.VMEM
    D = pltpu.SemaphoreType.DMA
    scratch = [
        V((96, 1024), BF16), V((SLOTS_FC, ENC, CH), BF16), V((SLOTS_FC, CH, ENC), BF16),
        V((2, 128, ENC), F32), V((256, ENC), BF16), V((2, 128, ENC), F32),
        V((128, ENC), BF16), V((128, ENC), BF16), V((8, 16, ENC), BF16), V((8, 16, ENC), BF16),
        V((4, 2, 4, 96, 512), BF16), V((4, 2, 4, 48, 512), BF16), V((ENC, 512), BF16),
        V((2, 256, HID), BF16), V((HID, 512), BF16),
        V((2, 2, 128, 512), F32), V((2, 2, 128, 512), BF16),
        V((2, 128, ENC), BF16), V((2, 128, ENC), BF16), V((2, 128, ENC), F32),
        V((128, ENC), BF16), V((128, ENC), BF16), V((2, 2, 128, ENC), BF16), V((ENC, 512), BF16),
        V((2, 2, 128, 512), BF16),
        V((1416, 512), F32), V((4, 4, 288, 512), BF16), V((2, 4, 144, 512), BF16), V((2, 4, 288, 512), BF16),
        V((3, 288, 512), BF16), V((3, 288, 512), BF16), V((288, 512), F32),
        V((3, 80, 512), BF16), V((3, 80, 512), BF16),
        V((4, 256, 768), BF16), V((4, 256, 768), BF16), V((4, 256, 768), BF16),
        D((2, NCH)), D((7,)), D((27,)), D((27,)), D((27,)), D((27,)),
        D((6,)), D((6,)), D((8,)), D((8,)), D((30,)), D((30,)), D((2,)), D((2,)),
    ]
    zs, zr, in_grad, out_grad = pl.pallas_call(
        kernel,
        out_shape=(
            jax.ShapeDtypeStruct((256, HID), BF16),
            jax.ShapeDtypeStruct((256, HID), BF16),
            jax.ShapeDtypeStruct((48, 1024), F32),
            jax.ShapeDtypeStruct((22, 1024), F32),
        ),
        in_specs=[vm] * 4 + [pl.BlockSpec(memory_space=pltpu.SMEM)] + [vm] * 2 + [anyspace] * 3,
        out_specs=(anyspace, anyspace, vm, vm),
        scratch_shapes=scratch,
        compiler_params=pltpu.CompilerParams(
            collective_id=0, has_side_effects=True, vmem_limit_bytes=62 << 20
        ),
        name="fused",
    )(
        enc_input, patch_order, norm_gain, final_gain, timestep,
        proj_in, proj_out, hidden_states, fc_in, fc_out,
    )
    state_grad = zs.astype(F32) + zr.astype(F32)
    return (state_grad, in_grad, out_grad)


def solution(mesh):
    in_specs = (
        P(("dp", "seq"), None),
        P(),
        P(None, "tensor"),
        P("tensor", None),
        P(),
        P(("dp", "seq"), None),
        P("dp"),
        P(),
        P("seq", "tensor"),
        P("seq", "tensor"),
    )
    out_specs = (P(("dp", "seq"), None), P(("dp", "seq"), "tensor"), P(("dp", "seq"), "tensor"))
    return jax.shard_map(
        on_device, mesh=mesh, in_specs=in_specs, out_specs=out_specs, check_vma=False
    )
```

```python
import functools
import math

import jax
import jax.numpy as jnp
from jax import lax
from jax.experimental import pallas as pl
from jax.experimental.pallas import tpu as pltpu
from jax.sharding import PartitionSpec as P

TSTEPS = 1000
MESH = pl.DeviceIdType.MESH
F32 = jnp.float32
BF16 = jnp.bfloat16
ENC = 1408
HID = 3072
CH = 512
NCH = 6
SLOTS_FC = 3


def dot(a, b):
    return jnp.dot(a, b, preferred_element_type=F32)


def dot_t(a, b):
    return lax.dot_general(a, b, (((1,), (1,)), ((), ())), preferred_element_type=F32)


def layer_norm(values, gain):
    center = jnp.mean(values, axis=-1, keepdims=True)
    square = jnp.mean(values * values, axis=-1, keepdims=True)
    return (values - center) * lax.rsqrt(square - center * center + 1e-06) * gain


def kernel(
    enc, order, ng, fg, steps, wi, wo_raw, hid, fcin, fcout,
    zs_out, zr_out, in_out, out_out,
    wo, fin_b, fout_b, x_s, normed, acc, fsend, frecv, feats, target,
    win, wob, wout, hid_all, hid_t,
    pre, pact, ps, pr, predo, pzs, pzr, dp_all, dp_t, dpre,
    og, gbuf, rh, r1, s2, r2, fin, cs, cr, ss_b, sr_b, zbuf,
    fsem, lsem, asem_s, asem_r, bsem_s, bsem_r, xs, xr, ts_, tr_, gs, gr, hs, hr,
):
    x = lax.axis_index("dp")
    s = lax.axis_index("seq")
    t = lax.axis_index("tensor")
    y = s // 4
    zl = (s // 2) % 2
    c = s % 2
    q = s // 2

    def dev(x_, y_, zl_, c_, t_):
        return (x_, y_ * 4 + zl_ * 2 + c_, t_)

    sib = dev(x, y, zl, 1 - c, t)
    zpart = dev(x, y, zl, c, 1 - t)
    zlpart = dev(x, y, 1 - zl, c, t)

    def heavy(d):
        return dev((x + d * (1 - c)) % 4, (y + d * c) % 4, zl, c, t)

    def light(d):
        return dev((x + d * c) % 4, (y + d * (1 - c)) % 4, zl, c, t)

    hc = x * (1 - c) + y * c
    lc = y * (1 - c) + x * c

    def rcopy(src, dst, send, recv, to):
        return pltpu.make_async_remote_copy(
            src_ref=src, dst_ref=dst, send_sem=send, recv_sem=recv, device_id=to, device_id_type=MESH
        )

    sent = []

    def go(src, dst, send, recv, to):
        cp = rcopy(src, dst, send, recv, to)
        cp.start()
        sent.append(cp)

    def got(dst, send, recv):
        rcopy(dst, dst, send, recv, sib).wait_recv()

    def fc_copies(j):
        return (
            pltpu.make_async_copy(
                fcin.at[:, pl.ds(j * CH, CH)], fin_b.at[j % SLOTS_FC], fsem.at[0, j]
            ),
            pltpu.make_async_copy(
                fcout.at[pl.ds(j * CH, CH)], fout_b.at[j % SLOTS_FC], fsem.at[1, j]
            ),
        )

    for j in range(SLOTS_FC):
        for cp in fc_copies(j):
            cp.start()
    hid_own = pltpu.make_async_copy(hid, hid_all.at[c], lsem.at[0])
    hid_own.start()

    wo[0:88] = wo_raw[...]
    wo[88:96] = jnp.zeros((8, 1024), BF16)

    bar = pltpu.get_barrier_semaphore()
    for d in range(1, 16):
        pl.semaphore_signal(bar, inc=1, device_id=(x, (s + d) % 16, t), device_id_type=MESH)
    for d in range(1, 4):
        pl.semaphore_signal(bar, inc=1, device_id=((x + d) % 4, s, t), device_id_type=MESH)
    pl.semaphore_signal(bar, inc=1, device_id=zpart, device_id_type=MESH)

    onehot = (lax.broadcasted_iota(jnp.int32, (256, 256), 0) == order[...].reshape(1, 256)).astype(F32)
    xin = dot(onehot.T.astype(BF16), enc[...])
    xin = jnp.swapaxes(xin.reshape(8, 2, 16, ENC), 0, 1).reshape(256, ENC)
    x_s[...] = xin.reshape(2, 128, ENC)
    normed[...] = layer_norm(xin, ng[...].reshape(1, ENC)).astype(BF16)
    acc[...] = jnp.zeros_like(acc)

    pl.semaphore_wait(bar, 19)

    is_src = c == x // 2

    class Gather:
        def __init__(self, src, buf, rows, ssem, rsem, lsem_):
            self.src, self.buf, self.rows, self.ss, self.rs, self.ls = src, buf, rows, ssem, rsem, lsem_

        def piece(self, da, db, z):
            yy = (y + da * (1 - c) + db * c + 4) % 4
            xx = (x + da * c + db * (1 - c) + 4) % 4
            if z == 2:
                return self.buf.at[yy, :, xx]
            return self.buf.at[yy, zl if z == 0 else 1 - zl, xx]

        def half(self, h):
            n = self.rows
            return self.src.at[pl.ds(pl.multiple_of((x % 2) * n, n), n), pl.ds(pl.multiple_of(h * 512, 512), 512)]

        def zero_copies(self):
            own = self.piece(0, 0, 0)
            return (
                rcopy(self.half(1 - c), own, self.ss.at[0], self.rs.at[0], sib),
                rcopy(self.half(0), own, self.ss.at[1], self.rs.at[1], dev(x, y, 1 - zl, 0, t)),
                rcopy(self.half(1), own, self.ss.at[2], self.rs.at[1], dev(x, y, 1 - zl, 1, t)),
            )

        def local(self):
            return pltpu.make_async_copy(self.half(c), self.piece(0, 0, 0), self.ls)

        def start0(self):
            @pl.when(is_src)
            def _():
                for cp in self.zero_copies():
                    cp.start()
                self.local().start()

        def end0(self):
            @pl.when(is_src)
            def _():
                for cp in self.zero_copies():
                    cp.wait_send()

        def put(self, n, ref, to):
            go(ref, ref, self.ss.at[n], self.rs.at[n], to)

        def take(self, n, ref):
            got(ref, self.ss.at[n], self.rs.at[n])

        def native(self):
            @pl.when(is_src)
            def _():
                self.local().wait()

            @pl.when(jnp.logical_not(is_src))
            def _():
                self.take(0, self.piece(0, 0, 0))

            self.begin(0)

        def foreign(self):
            self.take(1, self.piece(0, 0, 1))
            self.begin(1)

        def begin(self, z):
            own = self.piece(0, 0, z)
            self.put(3 + 4 * z, own, light(1))
            self.put(4 + 4 * z, own, light(3))
            self.put(11 + z, own, light(2))
            self.put(5 + 4 * z, own, heavy(1))
            self.put(6 + 4 * z, own, heavy(3))

        def light_near(self):
            self.take(3, self.piece(-1, 0, 0))
            self.take(8, self.piece(1, 0, 1))
            self.take(7, self.piece(-1, 0, 1))
            self.take(4, self.piece(1, 0, 0))
            for k, da in ((13, -1), (15, 1)):
                self.put(k, self.piece(da, 0, 2), heavy(1))
                self.put(k + 1, self.piece(da, 0, 2), heavy(3))

        def light_far(self):
            self.take(11, self.piece(2, 0, 0))
            self.take(12, self.piece(2, 0, 1))
            self.put(17, self.piece(2, 0, 2), heavy(1))
            self.put(18, self.piece(2, 0, 2), heavy(3))
            self.put(25, self.piece(2, 0, 2), heavy(2))

        def heavy_own(self):
            self.take(5, self.piece(0, -1, 0))
            self.put(19, self.piece(0, -1, 0), heavy(1))
            self.take(10, self.piece(0, 1, 1))
            self.put(20, self.piece(0, 1, 1), heavy(3))

        def heavy_other(self, i):
            da = (-1, 1)[i]
            self.take(13 + 2 * i, self.piece(da, -1, 2))
            self.put(21 + 2 * i, self.piece(da, -1, 0), heavy(1))
            self.take(14 + 2 * i, self.piece(da, 1, 2))
            self.put(22 + 2 * i, self.piece(da, 1, 1), heavy(3))

        def finish(self):
            self.take(9, self.piece(0, -1, 1))
            self.take(6, self.piece(0, 1, 0))
            for k, da in ((19, 0), (21, -1), (23, 1)):
                self.take(k, self.piece(da, 2, 0))
                self.take(k + 1, self.piece(da, 2, 1))
            for k, db in ((17, -1), (18, 1), (25, 2)):
                self.take(k, self.piece(2, db, 2))

    gi = Gather(wi, win, 96, asem_s, asem_r, lsem.at[1])
    go_ = Gather(wo, wob, 48, bsem_s, bsem_r, lsem.at[2])
    both = (gi, go_)
    for g in both:
        g.start0()
    go(hid, hid_all.at[c], hs.at[0], hr.at[0], sib)

    def ffn(j):
        for cp in fc_copies(j):
            cp.wait()
        h = dot(normed[...], fin_b[j % SLOTS_FC])
        a = (0.5 * h * (1.0 + lax.erf(h * math.sqrt(0.5)))).astype(BF16)
        acc[...] += dot(a, fout_b[j % SLOTS_FC]).reshape(2, 128, ENC)
        if j + SLOTS_FC < NCH:
            for cp in fc_copies(j + SLOTS_FC):
                cp.start()

    for g in both:
        g.native()
    for g in both:
        g.foreign()
    ffn(0)
    gi.light_near()
    ffn(1)
    gi.light_far()
    go_.light_near()
    ffn(2)
    gi.heavy_own()
    go_.light_far()
    ffn(3)
    gi.heavy_other(0)
    ffn(4)
    gi.heavy_other(1)
    ffn(5)
    fsend[...] = acc[1 - t].astype(BF16)
    go(fsend, frecv, hs.at[1], hr.at[1], zpart)
    go_.heavy_own()
    hid_own.wait()
    got(hid_all.at[1 - c], hs.at[0], hr.at[0])
    for p in range(2):
        for j in range(6):
            hid_t[j * 512:(j + 1) * 512, p * 256:(p + 1) * 256] = hid_all[p, :, j * 512:(j + 1) * 512].T
    go_.heavy_other(0)
    go_.heavy_other(1)
    gi.finish()

    for p in range(2):
        for n in range(2):
            cols = slice(n * 256, n * 256 + 256)
            v = dot(hid_all[p], win[:, :, :, :, cols].reshape(HID, 256))
            a = (v * jax.nn.sigmoid(v)).astype(BF16)
            for h in range(2):
                pre[h, p, :, cols] = v[h * 128:h * 128 + 128]
                pact[h, p, :, cols] = a[h * 128:h * 128 + 128]
    go_.finish()
    wout[...] = jnp.concatenate(
        [wob[i, z, 2 * k:2 * k + 2].reshape(96, 512)[0:88].astype(F32) for i in range(4) for z in range(2) for k in range(2)],
        axis=0,
    ).astype(BF16)
    v = dot_t(pact[1 - c].reshape(256, 512), wout[...]).astype(BF16).reshape(2, 128, ENC)
    ps[...] = v
    go(ps.at[1 - t], pr.at[1 - t], xs.at[0], xr.at[0], sib)
    go(ps.at[t], pr.at[t], xs.at[1], xr.at[1], sib)
    predo[...] = dot_t(pact[c].reshape(256, 512), wout[...]).reshape(2, 128, ENC)
    got(frecv, hs.at[1], hr.at[1])
    resid = x_s[t] + (acc[t] + frecv[...].astype(F32))
    feats[...] = layer_norm(resid, fg[...].reshape(1, ENC)).astype(BF16).reshape(8, 16, ENC)
    hi = s // 8
    for i in range(8):
        to = 2 * i + hi

        @pl.when(to == s)
        def _():
            pltpu.make_async_copy(feats.at[i], target.at[s % 8], ts_.at[i]).start()

        @pl.when(to != s)
        def _():
            rcopy(feats.at[i], target.at[s % 8], ts_.at[i], tr_.at[s % 8], (x, to, t)).start()

    got(pr.at[1 - t], xs.at[0], xr.at[0])
    pzs[...] = (predo[1 - t] + pr[1 - t].astype(F32)).astype(BF16)
    go(pzs, pzr, xs.at[2], xr.at[2], zpart)
    for i in range(8):
        to = 2 * i + hi

        @pl.when(to == s)
        def _():
            pltpu.make_async_copy(feats.at[i], target.at[s % 8], ts_.at[i]).wait()

        @pl.when(to != s)
        def _():
            rcopy(feats.at[i], target.at[s % 8], ts_.at[i], tr_.at[s % 8], (x, to, t)).wait_send()

    for i in range(8):
        @pl.when(c * 8 + i != s)
        def _():
            got(target.at[i], ts_.at[i], tr_.at[i])

    tgt = target[...].reshape(128, ENC).astype(F32)
    inv_target = lax.rsqrt(jnp.sum(tgt * tgt, axis=1, keepdims=True) + 1e-06)
    got(pr.at[t], xs.at[1], xr.at[1])
    got(pzr, xs.at[2], xr.at[2])
    pred = predo[t] + pr[t].astype(F32) + pzr[...].astype(F32)
    inv_pred = lax.rsqrt(jnp.sum(pred * pred, axis=1, keepdims=True) + 1e-06)
    cosine = jnp.sum(pred * tgt, axis=1, keepdims=True) * inv_pred * inv_target
    weight = (0.5 + steps[0].astype(F32) / TSTEPS) * ENC
    dp_all[c, t] = (
        -weight * (inv_target * inv_pred * tgt - cosine * inv_pred * inv_pred * pred)
    ).astype(BF16)
    go(dp_all.at[c, t], dp_all.at[c, t], xs.at[3], xr.at[3], zpart)
    go(dp_all.at[c, t], dp_all.at[c, t], xs.at[4], xr.at[4], sib)

    def back(h, p):
        d = dp_all[h, p]
        dp_t[:, pl.ds(pl.multiple_of((h * 2 + p) * 128, 128), 128)] = d.T
        dact = dot(d, wout[...])
        v = pre[h, p]
        sigma = jax.nn.sigmoid(v)
        dpre[p, h] = (dact * sigma * (1.0 + v * (1.0 - sigma))).astype(BF16)

    def win_rows(j):
        return win[j].reshape(768, 512)

    def to_sib(j):
        return rcopy(ss_b.at[j], sr_b.at[j], gs.at[j], gr.at[j], sib)

    def to_pair(j):
        return rcopy(zbuf.at[j], zr_out.at[:, pl.ds(j * 768, 768)], gs.at[4 + j], gr.at[4 + j], zpart)

    def keep(j):
        return pltpu.make_async_copy(zbuf.at[j], zs_out.at[:, pl.ds(j * 768, 768)], lsem.at[3 + j])

    def theirs():
        for j in range(4):
            ss_b[j] = dot_t(dpre[1 - c].reshape(256, 512), win_rows(j)).astype(BF16)
            to_sib(j).start()

    def ours():
        for j in range(4):
            v = dot_t(dpre[c].reshape(256, 512), win_rows(j))
            got(sr_b.at[j], gs.at[j], gr.at[j])
            zbuf[j] = (v + sr_b[j].astype(F32)).astype(BF16)

    def send_ours():
        for j in range(4):
            to_pair(j).start()
            keep(j).start()

    early = c == t
    back(c, t)
    got(dp_all.at[1 - c, t], xs.at[4], xr.at[4])
    back(1 - c, t)

    @pl.when(jnp.logical_not(early))
    def _():
        theirs()

    @pl.when(early)
    def _():
        ours()

    got(dp_all.at[c, 1 - t], xs.at[3], xr.at[3])
    go(dp_all.at[c, 1 - t], dp_all.at[c, 1 - t], xs.at[5], xr.at[5], sib)

    @pl.when(early)
    def _():
        send_ours()

    back(c, 1 - t)
    got(dp_all.at[1 - c, 1 - t], xs.at[5], xr.at[5])
    back(1 - c, 1 - t)

    @pl.when(early)
    def _():
        theirs()

    og[pl.ds(1408, 8)] = jnp.zeros((8, 512), F32)
    for i in range(4):
        og[i * 352:(i + 1) * 352] = dot(dp_t[i * 352:(i + 1) * 352], pact[...].reshape(512, 512))

    def grad(dh, dl):
        h = (hc + dh) % 4
        l = (lc + dl) % 4
        gidx = (h * (1 - c) + l * c) * 4 + l * (1 - c) + h * c
        rows = hid_t[pl.ds(pl.multiple_of(gidx * 192, 192), 192)]
        gbuf[h, l, 0:192] = dot(rows, dpre[...].reshape(512, 512)).astype(BF16)
        gbuf[h, l, 192:288] = og[pl.ds(pl.multiple_of(gidx * 88, 8), 96)].astype(BF16)
        return h, l

    lorder = (2, 1, 3, 0)
    for e in range(4):
        dl = lorder[e]
        h, l = grad(2, dl)
        go(gbuf.at[h, l, pl.ds(0, 144)], rh.at[0, dl], gs.at[8 + 4 * e], gr.at[8 + 4 * e], heavy(1))
        go(gbuf.at[h, l, pl.ds(144, 144)], rh.at[1, dl], gs.at[9 + 4 * e], gr.at[9 + 4 * e], heavy(3))

    @pl.when(jnp.logical_not(early))
    def _():
        ours()
        send_ours()

    for e in range(4):
        dl = lorder[e]
        for k, dh in ((0, 1), (1, 3)):
            h, l = grad(dh, dl)
            part = pl.ds(k * 144, 144)
            n = 8 + 4 * e + k
            got(rh.at[k, dl], gs.at[n], gr.at[n])
            gbuf[h, l, part] = (gbuf[h, l, part].astype(F32) + rh[k, dl].astype(F32)).astype(BF16)
            go(gbuf.at[h, l], r1.at[k, dl], gs.at[n + 2], gr.at[n + 2], heavy(dh))
    for e in range(4):
        dl = lorder[e]
        h, l = grad(0, dl)
        total = gbuf[h, l].astype(F32)
        for k in range(2):
            n = 10 + 4 * e + k
            got(r1.at[k, dl], gs.at[n], gr.at[n])
            total += r1[k, dl].astype(F32)
        if dl:
            s2[dl - 1] = total.astype(BF16)
            go(s2.at[dl - 1], r2.at[dl - 1], gs.at[23 + dl], gr.at[23 + dl], light(dl))
        else:
            fin[...] = total
    for dl in (2, 1, 3):
        got(r2.at[dl - 1], gs.at[23 + dl], gr.at[23 + dl])
        fin[...] += r2[dl - 1].astype(F32)

    def rows_for(zl_, c_):
        even = c_ == 0
        lo = jnp.where(even, fin[192:214], fin[214:236])
        hi_ = jnp.where(even, fin[236:258], fin[258:280])
        return fin[pl.ds(pl.multiple_of(zl_ * 96 + c_ * 48, 48), 48)], jnp.where(zl_ == 0, lo, hi_)

    dests = ((1 - zl, 1 - c), (1 - zl, c), (zl, 1 - c))
    for k in range(3):
        a, b = rows_for(*dests[k])
        cs[k, 0:48] = a.astype(BF16)
        cs[k, 48:80] = jnp.concatenate([b, jnp.zeros((10, 512), F32)], axis=0).astype(BF16)
        go(cs.at[k], cr.at[k], gs.at[27 + k], gr.at[27 + k], dev(x, y, dests[k][0], dests[k][1], t))
    factor = 1.0 / 128.0
    mine = pl.ds(pl.multiple_of(c * 512, 512), 512)
    other = pl.ds(pl.multiple_of((1 - c) * 512, 512), 512)
    a, b = rows_for(zl, c)
    for k in range(3):
        got(cr.at[k], gs.at[27 + k], gr.at[27 + k])
    in_out[:, mine] = (a + cr[1, 0:48].astype(F32)) * factor
    out_out[:, mine] = (b + cr[1, 48:80].astype(F32)[0:22]) * factor
    in_out[:, other] = (cr[0, 0:48].astype(F32) + cr[2, 0:48].astype(F32)) * factor
    out_out[:, other] = (cr[0, 48:80].astype(F32) + cr[2, 48:80].astype(F32))[0:22] * factor

    for j in range(4):
        to_pair(j).wait_recv()
        to_pair(j).wait_send()
        to_sib(j).wait_send()
        keep(j).wait()
    for g in both:
        g.end0()
    for cp in sent:
        cp.wait_send()


def close_kernel(a, b, in_ref, out_ref, state, in_grad, out_grad):
    state[...] = a[...].astype(F32) + b[...].astype(F32)

    @pl.when(pl.program_id(0) == 0)
    def _():
        in_grad[...] = in_ref[...]
        out_grad[...] = out_ref[...]


def close(a, b, in_grad, out_grad):
    rows = pl.BlockSpec((64, HID), lambda i: (i, 0))
    whole = [pl.BlockSpec(v.shape, lambda i: (0, 0)) for v in (in_grad, out_grad)]
    return pl.pallas_call(
        close_kernel,
        grid=(4,),
        out_shape=(
            jax.ShapeDtypeStruct((256, HID), F32),
            jax.ShapeDtypeStruct(in_grad.shape, F32),
            jax.ShapeDtypeStruct(out_grad.shape, F32),
        ),
        in_specs=[rows, rows] + whole,
        out_specs=(rows, *whole),
        name="close",
    )(a, b, in_grad, out_grad)


def on_device(
    enc_input, norm_gain, fc_in, fc_out, final_gain, hidden_states, timestep, patch_order, proj_in, proj_out
):
    vm = pl.BlockSpec(memory_space=pltpu.VMEM)
    anyspace = pl.BlockSpec(memory_space=pl.ANY)
    V = pltpu.VMEM
    D = pltpu.SemaphoreType.DMA
    scratch = [
        V((96, 1024), BF16), V((SLOTS_FC, ENC, CH), BF16), V((SLOTS_FC, CH, ENC), BF16),
        V((2, 128, ENC), F32), V((256, ENC), BF16), V((2, 128, ENC), F32),
        V((128, ENC), BF16), V((128, ENC), BF16), V((8, 16, ENC), BF16), V((8, 16, ENC), BF16),
        V((4, 2, 4, 96, 512), BF16), V((4, 2, 4, 48, 512), BF16), V((ENC, 512), BF16),
        V((2, 256, HID), BF16), V((HID, 512), BF16),
        V((2, 2, 128, 512), F32), V((2, 2, 128, 512), BF16),
        V((2, 128, ENC), BF16), V((2, 128, ENC), BF16), V((2, 128, ENC), F32),
        V((128, ENC), BF16), V((128, ENC), BF16), V((2, 2, 128, ENC), BF16), V((ENC, 512), BF16),
        V((2, 2, 128, 512), BF16),
        V((1416, 512), F32), V((4, 4, 288, 512), BF16), V((2, 4, 144, 512), BF16), V((2, 4, 288, 512), BF16),
        V((3, 288, 512), BF16), V((3, 288, 512), BF16), V((288, 512), F32),
        V((3, 80, 512), BF16), V((3, 80, 512), BF16),
        V((4, 256, 768), BF16), V((4, 256, 768), BF16), V((4, 256, 768), BF16),
        D((2, NCH)), D((7,)), D((26,)), D((26,)), D((26,)), D((26,)),
        D((6,)), D((6,)), D((8,)), D((8,)), D((30,)), D((30,)), D((2,)), D((2,)),
    ]
    zs, zr, in_grad, out_grad = pl.pallas_call(
        kernel,
        out_shape=(
            jax.ShapeDtypeStruct((256, HID), BF16),
            jax.ShapeDtypeStruct((256, HID), BF16),
            jax.ShapeDtypeStruct((48, 1024), F32),
            jax.ShapeDtypeStruct((22, 1024), F32),
        ),
        in_specs=[vm] * 4 + [pl.BlockSpec(memory_space=pltpu.SMEM)] + [vm] * 2 + [anyspace] * 3,
        out_specs=(anyspace, anyspace, vm, vm),
        scratch_shapes=scratch,
        compiler_params=pltpu.CompilerParams(
            collective_id=0, has_side_effects=True, vmem_limit_bytes=62 << 20
        ),
        name="fused",
    )(
        enc_input, patch_order, norm_gain, final_gain, timestep,
        proj_in, proj_out, hidden_states, fc_in, fc_out,
    )
    return close(zs, zr, in_grad, out_grad)


def solution(mesh):
    in_specs = (
        P(("dp", "seq"), None),
        P(),
        P(None, "tensor"),
        P("tensor", None),
        P(),
        P(("dp", "seq"), None),
        P("dp"),
        P(),
        P("seq", "tensor"),
        P("seq", "tensor"),
    )
    out_specs = (P(("dp", "seq"), None), P(("dp", "seq"), "tensor"), P(("dp", "seq"), "tensor"))
    return jax.shard_map(
        on_device, mesh=mesh, in_specs=in_specs, out_specs=out_specs, check_vma=False
    )
```

```python
import functools
import math

import jax
import jax.numpy as jnp
from jax import lax
from jax.experimental import pallas as pl
from jax.experimental.pallas import tpu as pltpu
from jax.sharding import PartitionSpec as P

TSTEPS = 1000
MESH = pl.DeviceIdType.MESH
F32 = jnp.float32
BF16 = jnp.bfloat16
ENC = 1408
HID = 3072
CH = 512
NCH = 6
SLOTS_FC = 3


def dot(a, b):
    return jnp.dot(a, b, preferred_element_type=F32)


def dot_t(a, b):
    return lax.dot_general(a, b, (((1,), (1,)), ((), ())), preferred_element_type=F32)


def layer_norm(values, gain):
    center = jnp.mean(values, axis=-1, keepdims=True)
    square = jnp.mean(values * values, axis=-1, keepdims=True)
    return (values - center) * lax.rsqrt(square - center * center + 1e-06) * gain


def kernel(
    enc, order, ng, fg, steps, wi, wo_raw, hid, fcin, fcout,
    zs_out, zr_out, in_out, out_out,
    wo, fin_b, fout_b, x_s, normed, acc, fsend, frecv, feats, target,
    win, wob, wout, hid_all, hid_t,
    pre, pact, ps, pr, predo, pzs, pzr, dp_all, dp_t, dpre,
    og, gbuf, rh, r1, s2, r2, fin, cs, cr, ss_b, sr_b, zbuf,
    fsem, lsem, asem_s, asem_r, bsem_s, bsem_r, xs, xr, ts_, tr_, gs, gr, hs, hr,
):
    x = lax.axis_index("dp")
    s = lax.axis_index("seq")
    t = lax.axis_index("tensor")
    y = s // 4
    zl = (s // 2) % 2
    c = s % 2
    q = s // 2

    def dev(x_, y_, zl_, c_, t_):
        return (x_, y_ * 4 + zl_ * 2 + c_, t_)

    sib = dev(x, y, zl, 1 - c, t)
    zpart = dev(x, y, zl, c, 1 - t)
    zlpart = dev(x, y, 1 - zl, c, t)

    def heavy(d):
        return dev((x + d * (1 - c)) % 4, (y + d * c) % 4, zl, c, t)

    def light(d):
        return dev((x + d * c) % 4, (y + d * (1 - c)) % 4, zl, c, t)

    hc = x * (1 - c) + y * c
    lc = y * (1 - c) + x * c

    def rcopy(src, dst, send, recv, to):
        return pltpu.make_async_remote_copy(
            src_ref=src, dst_ref=dst, send_sem=send, recv_sem=recv, device_id=to, device_id_type=MESH
        )

    sent = []

    def go(src, dst, send, recv, to):
        cp = rcopy(src, dst, send, recv, to)
        cp.start()
        sent.append(cp)

    def got(dst, send, recv):
        rcopy(dst, dst, send, recv, sib).wait_recv()

    def fc_copies(j):
        return (
            pltpu.make_async_copy(
                fcin.at[:, pl.ds(j * CH, CH)], fin_b.at[j % SLOTS_FC], fsem.at[0, j]
            ),
            pltpu.make_async_copy(
                fcout.at[pl.ds(j * CH, CH)], fout_b.at[j % SLOTS_FC], fsem.at[1, j]
            ),
        )

    for j in range(SLOTS_FC):
        for cp in fc_copies(j):
            cp.start()
    hid_own = pltpu.make_async_copy(hid, hid_all.at[c], lsem.at[0])
    hid_own.start()

    wo[0:88] = wo_raw[...]
    wo[88:96] = jnp.zeros((8, 1024), BF16)

    bar = pltpu.get_barrier_semaphore()
    for d in range(1, 16):
        pl.semaphore_signal(bar, inc=1, device_id=(x, (s + d) % 16, t), device_id_type=MESH)
    for d in range(1, 4):
        pl.semaphore_signal(bar, inc=1, device_id=((x + d) % 4, s, t), device_id_type=MESH)
    pl.semaphore_signal(bar, inc=1, device_id=zpart, device_id_type=MESH)

    onehot = (lax.broadcasted_iota(jnp.int32, (256, 256), 0) == order[...].reshape(1, 256)).astype(F32)
    xin = dot(onehot.T.astype(BF16), enc[...])
    xin = jnp.swapaxes(xin.reshape(8, 2, 16, ENC), 0, 1).reshape(256, ENC)
    x_s[...] = xin.reshape(2, 128, ENC)
    normed[...] = layer_norm(xin, ng[...].reshape(1, ENC)).astype(BF16)
    acc[...] = jnp.zeros_like(acc)

    pl.semaphore_wait(bar, 19)

    is_src = c == x // 2

    class Gather:
        def __init__(self, src, buf, rows, ssem, rsem, lsem_):
            self.src, self.buf, self.rows, self.ss, self.rs, self.ls = src, buf, rows, ssem, rsem, lsem_

        def piece(self, da, db, z):
            yy = (y + da * (1 - c) + db * c + 4) % 4
            xx = (x + da * c + db * (1 - c) + 4) % 4
            if z == 2:
                return self.buf.at[yy, :, xx]
            return self.buf.at[yy, zl if z == 0 else 1 - zl, xx]

        def half(self, h):
            n = self.rows
            return self.src.at[pl.ds(pl.multiple_of((x % 2) * n, n), n), pl.ds(pl.multiple_of(h * 512, 512), 512)]

        def zero_copies(self):
            own = self.piece(0, 0, 0)
            return (
                rcopy(self.half(1 - c), own, self.ss.at[0], self.rs.at[0], sib),
                rcopy(self.half(0), own, self.ss.at[1], self.rs.at[1], dev(x, y, 1 - zl, 0, t)),
                rcopy(self.half(1), own, self.ss.at[2], self.rs.at[1], dev(x, y, 1 - zl, 1, t)),
            )

        def local(self):
            return pltpu.make_async_copy(self.half(c), self.piece(0, 0, 0), self.ls)

        def start0(self):
            @pl.when(is_src)
            def _():
                for cp in self.zero_copies():
                    cp.start()
                self.local().start()

        def end0(self):
            @pl.when(is_src)
            def _():
                for cp in self.zero_copies():
                    cp.wait_send()

        def put(self, n, ref, to):
            go(ref, ref, self.ss.at[n], self.rs.at[n], to)

        def take(self, n, ref):
            got(ref, self.ss.at[n], self.rs.at[n])

        def native(self):
            @pl.when(is_src)
            def _():
                self.local().wait()

            @pl.when(jnp.logical_not(is_src))
            def _():
                self.take(0, self.piece(0, 0, 0))

            self.begin(0)

        def foreign(self):
            self.take(1, self.piece(0, 0, 1))
            self.begin(1)

        def begin(self, z):
            own = self.piece(0, 0, z)
            self.put(3 + 4 * z, own, light(1))
            self.put(4 + 4 * z, own, light(3))
            self.put(11 + z, own, light(2))
            self.put(5 + 4 * z, own, heavy(1))
            self.put(6 + 4 * z, own, heavy(3))

        def light_near(self):
            self.take(3, self.piece(-1, 0, 0))
            self.take(8, self.piece(1, 0, 1))
            self.take(7, self.piece(-1, 0, 1))
            self.take(4, self.piece(1, 0, 0))
            for k, da in ((13, -1), (15, 1)):
                self.put(k, self.piece(da, 0, 2), heavy(1))
                self.put(k + 1, self.piece(da, 0, 2), heavy(3))

        def light_far(self):
            self.take(11, self.piece(2, 0, 0))
            self.take(12, self.piece(2, 0, 1))
            self.put(17, self.piece(2, 0, 2), heavy(1))
            self.put(18, self.piece(2, 0, 2), heavy(3))
            self.put(25, self.piece(2, 0, 2), heavy(2))

        def heavy_own(self):
            self.take(5, self.piece(0, -1, 0))
            self.put(19, self.piece(0, -1, 0), heavy(1))
            self.take(10, self.piece(0, 1, 1))
            self.put(20, self.piece(0, 1, 1), heavy(3))

        def heavy_other(self, i):
            da = (-1, 1)[i]
            self.take(13 + 2 * i, self.piece(da, -1, 2))
            self.put(21 + 2 * i, self.piece(da, -1, 0), heavy(1))
            self.take(14 + 2 * i, self.piece(da, 1, 2))
            self.put(22 + 2 * i, self.piece(da, 1, 1), heavy(3))

        def finish(self):
            self.take(9, self.piece(0, -1, 1))
            self.take(6, self.piece(0, 1, 0))
            for k, da in ((19, 0), (21, -1), (23, 1)):
                self.take(k, self.piece(da, 2, 0))
                self.take(k + 1, self.piece(da, 2, 1))
            for k, db in ((17, -1), (18, 1), (25, 2)):
                self.take(k, self.piece(2, db, 2))

    gi = Gather(wi, win, 96, asem_s, asem_r, lsem.at[1])
    go_ = Gather(wo, wob, 48, bsem_s, bsem_r, lsem.at[2])
    both = (gi, go_)
    for g in both:
        g.start0()
    go(hid, hid_all.at[c], hs.at[0], hr.at[0], sib)

    def ffn(j):
        for cp in fc_copies(j):
            cp.wait()
        h = dot(normed[...], fin_b[j % SLOTS_FC])
        a = (0.5 * h * (1.0 + lax.erf(h * math.sqrt(0.5)))).astype(BF16)
        acc[...] += dot(a, fout_b[j % SLOTS_FC]).reshape(2, 128, ENC)
        if j + SLOTS_FC < NCH:
            for cp in fc_copies(j + SLOTS_FC):
                cp.start()

    for g in both:
        g.native()
    for g in both:
        g.foreign()
    ffn(0)
    gi.light_near()
    ffn(1)
    gi.light_far()
    go_.light_near()
    ffn(2)
    gi.heavy_own()
    go_.light_far()
    ffn(3)
    gi.heavy_other(0)
    ffn(4)
    gi.heavy_other(1)
    ffn(5)
    fsend[...] = acc[1 - t].astype(BF16)
    go(fsend, frecv, hs.at[1], hr.at[1], zpart)
    go_.heavy_own()
    hid_own.wait()
    got(hid_all.at[1 - c], hs.at[0], hr.at[0])
    go_.heavy_other(0)
    go_.heavy_other(1)
    got(frecv, hs.at[1], hr.at[1])
    resid = x_s[t] + (acc[t] + frecv[...].astype(F32))
    feats[...] = layer_norm(resid, fg[...].reshape(1, ENC)).astype(BF16).reshape(8, 16, ENC)
    hi = s // 8
    for i in range(8):
        to = 2 * i + hi

        @pl.when(to == s)
        def _():
            pltpu.make_async_copy(feats.at[i], target.at[s % 8], ts_.at[i]).start()

        @pl.when(to != s)
        def _():
            rcopy(feats.at[i], target.at[s % 8], ts_.at[i], tr_.at[s % 8], (x, to, t)).start()

    gi.finish()

    for p in range(2):
        for n in range(2):
            cols = slice(n * 256, n * 256 + 256)
            v = dot(hid_all[p], win[:, :, :, :, cols].reshape(HID, 256))
            a = (v * jax.nn.sigmoid(v)).astype(BF16)
            for h in range(2):
                pre[h, p, :, cols] = v[h * 128:h * 128 + 128]
                pact[h, p, :, cols] = a[h * 128:h * 128 + 128]
    go_.finish()
    wout[...] = jnp.concatenate(
        [wob[i, z, 2 * k:2 * k + 2].reshape(96, 512)[0:88].astype(F32) for i in range(4) for z in range(2) for k in range(2)],
        axis=0,
    ).astype(BF16)
    ps[1 - t] = dot_t(pact[1 - c, 1 - t], wout[...]).astype(BF16)
    go(ps.at[1 - t], pr.at[1 - t], xs.at[0], xr.at[0], sib)
    predo[1 - t] = dot_t(pact[c, 1 - t], wout[...])
    ps[t] = dot_t(pact[1 - c, t], wout[...]).astype(BF16)
    go(ps.at[t], pr.at[t], xs.at[1], xr.at[1], sib)
    got(pr.at[1 - t], xs.at[0], xr.at[0])
    halves = (slice(0, 64), slice(64, 128))
    for r, rows in enumerate(halves):
        pzs[rows] = (predo[1 - t, rows] + pr[1 - t, rows].astype(F32)).astype(BF16)
        go(pzs.at[rows], pzr.at[rows], xs.at[2 + 4 * r], xr.at[2 + 4 * r], zpart)
    predo[t] = dot_t(pact[c, t], wout[...])
    for p in range(2):
        for j in range(6):
            hid_t[j * 512:(j + 1) * 512, p * 256:(p + 1) * 256] = hid_all[p, :, j * 512:(j + 1) * 512].T
    for i in range(8):
        to = 2 * i + hi

        @pl.when(to == s)
        def _():
            pltpu.make_async_copy(feats.at[i], target.at[s % 8], ts_.at[i]).wait()

        @pl.when(to != s)
        def _():
            rcopy(feats.at[i], target.at[s % 8], ts_.at[i], tr_.at[s % 8], (x, to, t)).wait_send()

    for i in range(8):
        @pl.when(c * 8 + i != s)
        def _():
            got(target.at[i], ts_.at[i], tr_.at[i])

    tgt = target[...].reshape(128, ENC).astype(F32)
    inv_target = lax.rsqrt(jnp.sum(tgt * tgt, axis=1, keepdims=True) + 1e-06)
    got(pr.at[t], xs.at[1], xr.at[1])
    weight = (0.5 + steps[0].astype(F32) / TSTEPS) * ENC
    for r, rows in enumerate(halves):
        got(pzr.at[rows], xs.at[2 + 4 * r], xr.at[2 + 4 * r])
        pred = predo[t, rows] + pr[t, rows].astype(F32) + pzr[rows].astype(F32)
        ry = lax.rsqrt(jnp.sum(pred * pred, axis=1, keepdims=True) + 1e-06)
        rz = inv_target[rows]
        cosine = jnp.sum(pred * tgt[rows], axis=1, keepdims=True) * ry * rz
        dp_all[c, t, rows] = (-weight * (rz * ry * tgt[rows] - cosine * ry * ry * pred)).astype(BF16)
        part = dp_all.at[c, t, rows]
        go(part, part, xs.at[3 + 4 * r], xr.at[3 + 4 * r], zpart)
    go(dp_all.at[c, t], dp_all.at[c, t], xs.at[4], xr.at[4], sib)

    def back(h, p):
        d = dp_all[h, p]
        dp_t[:, pl.ds(pl.multiple_of((h * 2 + p) * 128, 128), 128)] = d.T
        dact = dot(d, wout[...])
        v = pre[h, p]
        sigma = jax.nn.sigmoid(v)
        dpre[p, h] = (dact * sigma * (1.0 + v * (1.0 - sigma))).astype(BF16)

    def win_rows(j):
        return win[j].reshape(768, 512)

    def to_sib(j):
        return rcopy(ss_b.at[j], sr_b.at[j], gs.at[j], gr.at[j], sib)

    def to_pair(j):
        return rcopy(zbuf.at[j], zr_out.at[:, pl.ds(j * 768, 768)], gs.at[4 + j], gr.at[4 + j], zpart)

    def keep(j):
        return pltpu.make_async_copy(zbuf.at[j], zs_out.at[:, pl.ds(j * 768, 768)], lsem.at[3 + j])

    def theirs():
        for j in range(4):
            ss_b[j] = dot_t(dpre[1 - c].reshape(256, 512), win_rows(j)).astype(BF16)
            to_sib(j).start()

    def ours():
        for j in range(4):
            v = dot_t(dpre[c].reshape(256, 512), win_rows(j))
            got(sr_b.at[j], gs.at[j], gr.at[j])
            zbuf[j] = (v + sr_b[j].astype(F32)).astype(BF16)

    def send_ours():
        for j in range(4):
            to_pair(j).start()
            keep(j).start()

    early = c == t
    back(c, t)
    got(dp_all.at[1 - c, t], xs.at[4], xr.at[4])
    back(1 - c, t)

    @pl.when(jnp.logical_not(early))
    def _():
        theirs()

    @pl.when(early)
    def _():
        ours()

    for r, rows in enumerate(halves):
        part = dp_all.at[c, 1 - t, rows]
        got(part, xs.at[3 + 4 * r], xr.at[3 + 4 * r])
        go(part, part, xs.at[5 + 3 * r], xr.at[5 + 3 * r], sib)

    @pl.when(early)
    def _():
        send_ours()

    back(c, 1 - t)
    for r, rows in enumerate(halves):
        got(dp_all.at[1 - c, 1 - t, rows], xs.at[5 + 3 * r], xr.at[5 + 3 * r])
    back(1 - c, 1 - t)

    @pl.when(early)
    def _():
        theirs()

    og[pl.ds(1408, 8)] = jnp.zeros((8, 512), F32)
    for i in range(4):
        og[i * 352:(i + 1) * 352] = dot(dp_t[i * 352:(i + 1) * 352], pact[...].reshape(512, 512))

    def grad(dh, dl):
        h = (hc + dh) % 4
        l = (lc + dl) % 4
        gidx = (h * (1 - c) + l * c) * 4 + l * (1 - c) + h * c
        rows = hid_t[pl.ds(pl.multiple_of(gidx * 192, 192), 192)]
        gbuf[h, l, 0:192] = dot(rows, dpre[...].reshape(512, 512)).astype(BF16)
        gbuf[h, l, 192:288] = og[pl.ds(pl.multiple_of(gidx * 88, 8), 96)].astype(BF16)
        return h, l

    lorder = (2, 1, 3, 0)
    for e in range(4):
        dl = lorder[e]
        h, l = grad(2, dl)
        go(gbuf.at[h, l, pl.ds(0, 144)], rh.at[0, dl], gs.at[8 + 4 * e], gr.at[8 + 4 * e], heavy(1))
        go(gbuf.at[h, l, pl.ds(144, 144)], rh.at[1, dl], gs.at[9 + 4 * e], gr.at[9 + 4 * e], heavy(3))

    @pl.when(jnp.logical_not(early))
    def _():
        ours()
        send_ours()

    for e in range(4):
        dl = lorder[e]
        for k, dh in ((0, 1), (1, 3)):
            h, l = grad(dh, dl)
            part = pl.ds(k * 144, 144)
            n = 8 + 4 * e + k
            got(rh.at[k, dl], gs.at[n], gr.at[n])
            gbuf[h, l, part] = (gbuf[h, l, part].astype(F32) + rh[k, dl].astype(F32)).astype(BF16)
            go(gbuf.at[h, l], r1.at[k, dl], gs.at[n + 2], gr.at[n + 2], heavy(dh))
    for e in range(4):
        dl = lorder[e]
        h, l = grad(0, dl)
        total = gbuf[h, l].astype(F32)
        for k in range(2):
            n = 10 + 4 * e + k
            got(r1.at[k, dl], gs.at[n], gr.at[n])
            total += r1[k, dl].astype(F32)
        if dl:
            s2[dl - 1] = total.astype(BF16)
            go(s2.at[dl - 1], r2.at[dl - 1], gs.at[23 + dl], gr.at[23 + dl], light(dl))
        else:
            fin[...] = total
    for dl in (2, 1, 3):
        got(r2.at[dl - 1], gs.at[23 + dl], gr.at[23 + dl])
        fin[...] += r2[dl - 1].astype(F32)

    def rows_for(zl_, c_):
        even = c_ == 0
        lo = jnp.where(even, fin[192:214], fin[214:236])
        hi_ = jnp.where(even, fin[236:258], fin[258:280])
        return fin[pl.ds(pl.multiple_of(zl_ * 96 + c_ * 48, 48), 48)], jnp.where(zl_ == 0, lo, hi_)

    dests = ((1 - zl, 1 - c), (1 - zl, c), (zl, 1 - c))
    for k in range(3):
        a, b = rows_for(*dests[k])
        cs[k, 0:48] = a.astype(BF16)
        cs[k, 48:80] = jnp.concatenate([b, jnp.zeros((10, 512), F32)], axis=0).astype(BF16)
        go(cs.at[k], cr.at[k], gs.at[27 + k], gr.at[27 + k], dev(x, y, dests[k][0], dests[k][1], t))
    factor = 1.0 / 128.0
    mine = pl.ds(pl.multiple_of(c * 512, 512), 512)
    other = pl.ds(pl.multiple_of((1 - c) * 512, 512), 512)
    a, b = rows_for(zl, c)
    for k in range(3):
        got(cr.at[k], gs.at[27 + k], gr.at[27 + k])
    in_out[:, mine] = (a + cr[1, 0:48].astype(F32)) * factor
    out_out[:, mine] = (b + cr[1, 48:80].astype(F32)[0:22]) * factor
    in_out[:, other] = (cr[0, 0:48].astype(F32) + cr[2, 0:48].astype(F32)) * factor
    out_out[:, other] = (cr[0, 48:80].astype(F32) + cr[2, 48:80].astype(F32))[0:22] * factor

    for j in range(4):
        to_pair(j).wait_recv()
        to_pair(j).wait_send()
        to_sib(j).wait_send()
        keep(j).wait()
    for g in both:
        g.end0()
    for cp in sent:
        cp.wait_send()


def close_kernel(a, b, in_ref, out_ref, state, in_grad, out_grad):
    state[...] = a[...].astype(F32) + b[...].astype(F32)

    @pl.when(pl.program_id(0) == 0)
    def _():
        in_grad[...] = in_ref[...]
        out_grad[...] = out_ref[...]


def close(a, b, in_grad, out_grad):
    rows = pl.BlockSpec((128, HID), lambda i: (i, 0))
    whole = [pl.BlockSpec(v.shape, lambda i: (0, 0)) for v in (in_grad, out_grad)]
    return pl.pallas_call(
        close_kernel,
        grid=(2,),
        out_shape=(
            jax.ShapeDtypeStruct((256, HID), F32),
            jax.ShapeDtypeStruct(in_grad.shape, F32),
            jax.ShapeDtypeStruct(out_grad.shape, F32),
        ),
        in_specs=[rows, rows] + whole,
        out_specs=(rows, *whole),
        name="close",
    )(a, b, in_grad, out_grad)


def on_device(
    enc_input, norm_gain, fc_in, fc_out, final_gain, hidden_states, timestep, patch_order, proj_in, proj_out
):
    vm = pl.BlockSpec(memory_space=pltpu.VMEM)
    anyspace = pl.BlockSpec(memory_space=pl.ANY)
    V = pltpu.VMEM
    D = pltpu.SemaphoreType.DMA
    scratch = [
        V((96, 1024), BF16), V((SLOTS_FC, ENC, CH), BF16), V((SLOTS_FC, CH, ENC), BF16),
        V((2, 128, ENC), F32), V((256, ENC), BF16), V((2, 128, ENC), F32),
        V((128, ENC), BF16), V((128, ENC), BF16), V((8, 16, ENC), BF16), V((8, 16, ENC), BF16),
        V((4, 2, 4, 96, 512), BF16), V((4, 2, 4, 48, 512), BF16), V((ENC, 512), BF16),
        V((2, 256, HID), BF16), V((HID, 512), BF16),
        V((2, 2, 128, 512), F32), V((2, 2, 128, 512), BF16),
        V((2, 128, ENC), BF16), V((2, 128, ENC), BF16), V((2, 128, ENC), F32),
        V((128, ENC), BF16), V((128, ENC), BF16), V((2, 2, 128, ENC), BF16), V((ENC, 512), BF16),
        V((2, 2, 128, 512), BF16),
        V((1416, 512), F32), V((4, 4, 288, 512), BF16), V((2, 4, 144, 512), BF16), V((2, 4, 288, 512), BF16),
        V((3, 288, 512), BF16), V((3, 288, 512), BF16), V((288, 512), F32),
        V((3, 80, 512), BF16), V((3, 80, 512), BF16),
        V((4, 256, 768), BF16), V((4, 256, 768), BF16), V((4, 256, 768), BF16),
        D((2, NCH)), D((7,)), D((26,)), D((26,)), D((26,)), D((26,)),
        D((9,)), D((9,)), D((8,)), D((8,)), D((30,)), D((30,)), D((2,)), D((2,)),
    ]
    zs, zr, in_grad, out_grad = pl.pallas_call(
        kernel,
        out_shape=(
            jax.ShapeDtypeStruct((256, HID), BF16),
            jax.ShapeDtypeStruct((256, HID), BF16),
            jax.ShapeDtypeStruct((48, 1024), F32),
            jax.ShapeDtypeStruct((22, 1024), F32),
        ),
        in_specs=[vm] * 4 + [pl.BlockSpec(memory_space=pltpu.SMEM)] + [vm] * 2 + [anyspace] * 3,
        out_specs=(anyspace, anyspace, vm, vm),
        scratch_shapes=scratch,
        compiler_params=pltpu.CompilerParams(
            collective_id=0, has_side_effects=True, vmem_limit_bytes=62 << 20
        ),
        name="fused",
    )(
        enc_input, patch_order, norm_gain, final_gain, timestep,
        proj_in, proj_out, hidden_states, fc_in, fc_out,
    )
    return close(zs, zr, in_grad, out_grad)


def solution(mesh):
    in_specs = (
        P(("dp", "seq"), None),
        P(),
        P(None, "tensor"),
        P("tensor", None),
        P(),
        P(("dp", "seq"), None),
        P("dp"),
        P(),
        P("seq", "tensor"),
        P("seq", "tensor"),
    )
    out_specs = (P(("dp", "seq"), None), P(("dp", "seq"), "tensor"), P(("dp", "seq"), "tensor"))
    return jax.shard_map(
        on_device, mesh=mesh, in_specs=in_specs, out_specs=out_specs, check_vma=False
    )
```

```python
import functools
import math

import jax
import jax.numpy as jnp
from jax import lax
from jax.experimental import pallas as pl
from jax.experimental.pallas import tpu as pltpu
from jax.sharding import PartitionSpec as P

TSTEPS = 1000
MESH = pl.DeviceIdType.MESH
F32 = jnp.float32
BF16 = jnp.bfloat16
ENC = 1408
HID = 3072
CH = 512
NCH = 6
SLOTS_FC = 3


def dot(a, b):
    return jnp.dot(a, b, preferred_element_type=F32)


def dot_t(a, b):
    return lax.dot_general(a, b, (((1,), (1,)), ((), ())), preferred_element_type=F32)


def layer_norm(values, gain):
    center = jnp.mean(values, axis=-1, keepdims=True)
    square = jnp.mean(values * values, axis=-1, keepdims=True)
    return (values - center) * lax.rsqrt(square - center * center + 1e-06) * gain


def kernel(
    enc, order, ng, fg, steps, wi, wo_raw, hid, fcin, fcout,
    zs_out, zr_out, in_out, out_out,
    wo, fin_b, fout_b, x_s, normed, acc, fsend, frecv, feats, target,
    win, wob, wout, hid_all, hid_t,
    pre, pact, ps, pr, predo, pzs, pzr, dp_all, dp_t, dpre,
    og, gbuf, rh, r1, s2, r2, fin, cs, cr, ss_b, sr_b, zbuf,
    fsem, lsem, asem_s, asem_r, bsem_s, bsem_r, xs, xr, ts_, tr_, gs, gr, hs, hr,
):
    x = lax.axis_index("dp")
    s = lax.axis_index("seq")
    t = lax.axis_index("tensor")
    y = s // 4
    zl = (s // 2) % 2
    c = s % 2
    q = s // 2

    def dev(x_, y_, zl_, c_, t_):
        return (x_, y_ * 4 + zl_ * 2 + c_, t_)

    sib = dev(x, y, zl, 1 - c, t)
    zpart = dev(x, y, zl, c, 1 - t)
    zlpart = dev(x, y, 1 - zl, c, t)

    def heavy(d):
        return dev((x + d * (1 - c)) % 4, (y + d * c) % 4, zl, c, t)

    def light(d):
        return dev((x + d * c) % 4, (y + d * (1 - c)) % 4, zl, c, t)

    hc = x * (1 - c) + y * c
    lc = y * (1 - c) + x * c

    def rcopy(src, dst, send, recv, to):
        return pltpu.make_async_remote_copy(
            src_ref=src, dst_ref=dst, send_sem=send, recv_sem=recv, device_id=to, device_id_type=MESH
        )

    sent = []

    def go(src, dst, send, recv, to):
        cp = rcopy(src, dst, send, recv, to)
        cp.start()
        sent.append(cp)

    def got(dst, send, recv):
        rcopy(dst, dst, send, recv, sib).wait_recv()

    def fc_copies(j):
        return (
            pltpu.make_async_copy(
                fcin.at[:, pl.ds(j * CH, CH)], fin_b.at[j % SLOTS_FC], fsem.at[0, j]
            ),
            pltpu.make_async_copy(
                fcout.at[pl.ds(j * CH, CH)], fout_b.at[j % SLOTS_FC], fsem.at[1, j]
            ),
        )

    for j in range(SLOTS_FC):
        for cp in fc_copies(j):
            cp.start()
    hid_own = pltpu.make_async_copy(hid, hid_all.at[c], lsem.at[0])
    hid_own.start()

    wo[0:88] = wo_raw[...]
    wo[88:96] = jnp.zeros((8, 1024), BF16)

    bar = pltpu.get_barrier_semaphore()
    for d in range(1, 16):
        pl.semaphore_signal(bar, inc=1, device_id=(x, (s + d) % 16, t), device_id_type=MESH)
    for d in range(1, 4):
        pl.semaphore_signal(bar, inc=1, device_id=((x + d) % 4, s, t), device_id_type=MESH)
    pl.semaphore_signal(bar, inc=1, device_id=zpart, device_id_type=MESH)

    onehot = (lax.broadcasted_iota(jnp.int32, (256, 256), 0) == order[...].reshape(1, 256)).astype(F32)
    xin = dot(onehot.T.astype(BF16), enc[...])
    xin = jnp.swapaxes(xin.reshape(8, 2, 16, ENC), 0, 1).reshape(256, ENC)
    x_s[...] = xin.reshape(2, 128, ENC)
    normed[...] = layer_norm(xin, ng[...].reshape(1, ENC)).astype(BF16)
    acc[...] = jnp.zeros_like(acc)

    pl.semaphore_wait(bar, 19)

    is_src = c == x // 2

    class Gather:
        def __init__(self, src, buf, rows, ssem, rsem, lsem_):
            self.src, self.buf, self.rows, self.ss, self.rs, self.ls = src, buf, rows, ssem, rsem, lsem_

        def piece(self, da, db, z):
            yy = (y + da * (1 - c) + db * c + 4) % 4
            xx = (x + da * c + db * (1 - c) + 4) % 4
            if z == 2:
                return self.buf.at[yy, :, xx]
            return self.buf.at[yy, zl if z == 0 else 1 - zl, xx]

        def half(self, h):
            n = self.rows
            return self.src.at[pl.ds(pl.multiple_of((x % 2) * n, n), n), pl.ds(pl.multiple_of(h * 512, 512), 512)]

        def zero_copies(self):
            own = self.piece(0, 0, 0)
            return (
                rcopy(self.half(1 - c), own, self.ss.at[0], self.rs.at[0], sib),
                rcopy(self.half(0), own, self.ss.at[1], self.rs.at[1], dev(x, y, 1 - zl, 0, t)),
                rcopy(self.half(1), own, self.ss.at[2], self.rs.at[1], dev(x, y, 1 - zl, 1, t)),
            )

        def local(self):
            return pltpu.make_async_copy(self.half(c), self.piece(0, 0, 0), self.ls)

        def start0(self):
            @pl.when(is_src)
            def _():
                for cp in self.zero_copies():
                    cp.start()
                self.local().start()

        def end0(self):
            @pl.when(is_src)
            def _():
                for cp in self.zero_copies():
                    cp.wait_send()

        def put(self, n, ref, to):
            go(ref, ref, self.ss.at[n], self.rs.at[n], to)

        def take(self, n, ref):
            got(ref, self.ss.at[n], self.rs.at[n])

        def native(self):
            @pl.when(is_src)
            def _():
                self.local().wait()

            @pl.when(jnp.logical_not(is_src))
            def _():
                self.take(0, self.piece(0, 0, 0))

            self.begin(0)

        def foreign(self):
            self.take(1, self.piece(0, 0, 1))
            self.begin(1)

        def begin(self, z):
            own = self.piece(0, 0, z)
            self.put(3 + 4 * z, own, light(1))
            self.put(4 + 4 * z, own, light(3))
            self.put(11 + z, own, light(2))
            self.put(5 + 4 * z, own, heavy(1))
            self.put(6 + 4 * z, own, heavy(3))

        def light_near(self):
            self.take(3, self.piece(-1, 0, 0))
            self.take(8, self.piece(1, 0, 1))
            self.take(7, self.piece(-1, 0, 1))
            self.take(4, self.piece(1, 0, 0))
            for k, da in ((13, -1), (15, 1)):
                self.put(k, self.piece(da, 0, 2), heavy(1))
                self.put(k + 1, self.piece(da, 0, 2), heavy(3))

        def light_far(self):
            self.take(11, self.piece(2, 0, 0))
            self.take(12, self.piece(2, 0, 1))
            self.put(17, self.piece(2, 0, 2), heavy(1))
            self.put(18, self.piece(2, 0, 2), heavy(3))
            self.put(25, self.piece(2, 0, 2), heavy(2))

        def heavy_own(self):
            self.take(5, self.piece(0, -1, 0))
            self.put(19, self.piece(0, -1, 0), heavy(1))
            self.take(10, self.piece(0, 1, 1))
            self.put(20, self.piece(0, 1, 1), heavy(3))

        def heavy_other(self, i):
            da = (-1, 1)[i]
            self.take(13 + 2 * i, self.piece(da, -1, 2))
            self.put(21 + 2 * i, self.piece(da, -1, 0), heavy(1))
            self.take(14 + 2 * i, self.piece(da, 1, 2))
            self.put(22 + 2 * i, self.piece(da, 1, 1), heavy(3))

        def finish(self):
            self.take(9, self.piece(0, -1, 1))
            self.take(6, self.piece(0, 1, 0))
            for k, da in ((19, 0), (21, -1), (23, 1)):
                self.take(k, self.piece(da, 2, 0))
                self.take(k + 1, self.piece(da, 2, 1))
            for k, db in ((17, -1), (18, 1), (25, 2)):
                self.take(k, self.piece(2, db, 2))

    gi = Gather(wi, win, 96, asem_s, asem_r, lsem.at[1])
    go_ = Gather(wo, wob, 48, bsem_s, bsem_r, lsem.at[2])
    both = (gi, go_)
    for g in both:
        g.start0()
    go(hid, hid_all.at[c], hs.at[0], hr.at[0], sib)

    def ffn(j):
        for cp in fc_copies(j):
            cp.wait()
        h = dot(normed[...], fin_b[j % SLOTS_FC])
        a = (0.5 * h * (1.0 + lax.erf(h * math.sqrt(0.5)))).astype(BF16)
        acc[...] += dot(a, fout_b[j % SLOTS_FC]).reshape(2, 128, ENC)
        if j + SLOTS_FC < NCH:
            for cp in fc_copies(j + SLOTS_FC):
                cp.start()

    for g in both:
        g.native()
    for g in both:
        g.foreign()
    ffn(0)
    gi.light_near()
    gi.heavy_own()
    ffn(1)
    gi.light_far()
    go_.light_near()
    ffn(2)
    go_.light_far()
    ffn(3)
    gi.heavy_other(0)
    ffn(4)
    gi.heavy_other(1)
    ffn(5)
    fsend[...] = acc[1 - t].astype(BF16)
    go(fsend, frecv, hs.at[1], hr.at[1], zpart)
    go_.heavy_own()
    hid_own.wait()
    got(hid_all.at[1 - c], hs.at[0], hr.at[0])
    go_.heavy_other(0)
    go_.heavy_other(1)
    got(frecv, hs.at[1], hr.at[1])
    resid = x_s[t] + (acc[t] + frecv[...].astype(F32))
    feats[...] = layer_norm(resid, fg[...].reshape(1, ENC)).astype(BF16).reshape(8, 16, ENC)
    hi = s // 8
    for i in range(8):
        to = 2 * i + hi

        @pl.when(to == s)
        def _():
            pltpu.make_async_copy(feats.at[i], target.at[s % 8], ts_.at[i]).start()

        @pl.when(to != s)
        def _():
            rcopy(feats.at[i], target.at[s % 8], ts_.at[i], tr_.at[s % 8], (x, to, t)).start()

    gi.finish()

    for p in range(2):
        for n in range(2):
            cols = slice(n * 256, n * 256 + 256)
            v = dot(hid_all[p], win[:, :, :, :, cols].reshape(HID, 256))
            a = (v * jax.nn.sigmoid(v)).astype(BF16)
            for h in range(2):
                pre[h, p, :, cols] = v[h * 128:h * 128 + 128]
                pact[h, p, :, cols] = a[h * 128:h * 128 + 128]
    go_.finish()
    wout[...] = jnp.concatenate(
        [wob[i, z, 2 * k:2 * k + 2].reshape(96, 512)[0:88].astype(F32) for i in range(4) for z in range(2) for k in range(2)],
        axis=0,
    ).astype(BF16)
    ps[1 - t] = dot_t(pact[1 - c, 1 - t], wout[...]).astype(BF16)
    go(ps.at[1 - t], pr.at[1 - t], xs.at[0], xr.at[0], sib)
    predo[1 - t] = dot_t(pact[c, 1 - t], wout[...])
    ps[t] = dot_t(pact[1 - c, t], wout[...]).astype(BF16)
    go(ps.at[t], pr.at[t], xs.at[1], xr.at[1], sib)
    got(pr.at[1 - t], xs.at[0], xr.at[0])
    pieces = [slice(32 * r, 32 * r + 32) for r in range(4)]
    for r, rows in enumerate(pieces):
        pzs[rows] = (predo[1 - t, rows] + pr[1 - t, rows].astype(F32)).astype(BF16)
        go(pzs.at[rows], pzr.at[rows], xs.at[6 + r], xr.at[6 + r], zpart)
    predo[t] = dot_t(pact[c, t], wout[...])
    for p in range(2):
        for j in range(6):
            hid_t[j * 512:(j + 1) * 512, p * 256:(p + 1) * 256] = hid_all[p, :, j * 512:(j + 1) * 512].T
    for i in range(8):
        to = 2 * i + hi

        @pl.when(to == s)
        def _():
            pltpu.make_async_copy(feats.at[i], target.at[s % 8], ts_.at[i]).wait()

        @pl.when(to != s)
        def _():
            rcopy(feats.at[i], target.at[s % 8], ts_.at[i], tr_.at[s % 8], (x, to, t)).wait_send()

    for i in range(8):
        @pl.when(c * 8 + i != s)
        def _():
            got(target.at[i], ts_.at[i], tr_.at[i])

    tgt = target[...].reshape(128, ENC).astype(F32)
    inv_target = lax.rsqrt(jnp.sum(tgt * tgt, axis=1, keepdims=True) + 1e-06)
    got(pr.at[t], xs.at[1], xr.at[1])
    weight = (0.5 + steps[0].astype(F32) / TSTEPS) * ENC
    for r, rows in enumerate(pieces):
        got(pzr.at[rows], xs.at[6 + r], xr.at[6 + r])
        pred = predo[t, rows] + pr[t, rows].astype(F32) + pzr[rows].astype(F32)
        ry = lax.rsqrt(jnp.sum(pred * pred, axis=1, keepdims=True) + 1e-06)
        rz = inv_target[rows]
        cosine = jnp.sum(pred * tgt[rows], axis=1, keepdims=True) * ry * rz
        dp_all[c, t, rows] = (-weight * (rz * ry * tgt[rows] - cosine * ry * ry * pred)).astype(BF16)
        part = dp_all.at[c, t, rows]
        go(part, part, xs.at[10 + r], xr.at[10 + r], zpart)
    go(dp_all.at[c, t], dp_all.at[c, t], xs.at[4], xr.at[4], sib)

    def back(h, p):
        d = dp_all[h, p]
        dp_t[:, pl.ds(pl.multiple_of((h * 2 + p) * 128, 128), 128)] = d.T
        dact = dot(d, wout[...])
        v = pre[h, p]
        sigma = jax.nn.sigmoid(v)
        dpre[p, h] = (dact * sigma * (1.0 + v * (1.0 - sigma))).astype(BF16)

    def win_rows(j):
        return win[j].reshape(768, 512)

    def to_sib(j):
        return rcopy(ss_b.at[j], sr_b.at[j], gs.at[j], gr.at[j], sib)

    def to_pair(j):
        return rcopy(zbuf.at[j], zr_out.at[:, pl.ds(j * 768, 768)], gs.at[4 + j], gr.at[4 + j], zpart)

    def keep(j):
        return pltpu.make_async_copy(zbuf.at[j], zs_out.at[:, pl.ds(j * 768, 768)], lsem.at[3 + j])

    def theirs():
        for j in range(4):
            ss_b[j] = dot_t(dpre[1 - c].reshape(256, 512), win_rows(j)).astype(BF16)
            to_sib(j).start()

    def ours():
        for j in range(4):
            v = dot_t(dpre[c].reshape(256, 512), win_rows(j))
            got(sr_b.at[j], gs.at[j], gr.at[j])
            zbuf[j] = (v + sr_b[j].astype(F32)).astype(BF16)

    def send_ours():
        for j in range(4):
            to_pair(j).start()
            keep(j).start()

    early = c == t
    back(c, t)
    got(dp_all.at[1 - c, t], xs.at[4], xr.at[4])
    back(1 - c, t)

    @pl.when(jnp.logical_not(early))
    def _():
        theirs()

    @pl.when(early)
    def _():
        ours()

    for r, rows in enumerate(pieces):
        part = dp_all.at[c, 1 - t, rows]
        got(part, xs.at[10 + r], xr.at[10 + r])
        go(part, part, xs.at[14 + r], xr.at[14 + r], sib)

    @pl.when(early)
    def _():
        send_ours()

    back(c, 1 - t)
    for r, rows in enumerate(pieces):
        got(dp_all.at[1 - c, 1 - t, rows], xs.at[14 + r], xr.at[14 + r])
    back(1 - c, 1 - t)

    @pl.when(early)
    def _():
        theirs()

    og[pl.ds(1408, 8)] = jnp.zeros((8, 512), F32)
    for i in range(4):
        og[i * 352:(i + 1) * 352] = dot(dp_t[i * 352:(i + 1) * 352], pact[...].reshape(512, 512))

    def grad(dh, dl):
        h = (hc + dh) % 4
        l = (lc + dl) % 4
        gidx = (h * (1 - c) + l * c) * 4 + l * (1 - c) + h * c
        rows = hid_t[pl.ds(pl.multiple_of(gidx * 192, 192), 192)]
        gbuf[h, l, 0:192] = dot(rows, dpre[...].reshape(512, 512)).astype(BF16)
        gbuf[h, l, 192:288] = og[pl.ds(pl.multiple_of(gidx * 88, 8), 96)].astype(BF16)
        return h, l

    lorder = (2, 1, 3, 0)
    for e in range(4):
        dl = lorder[e]
        h, l = grad(2, dl)
        go(gbuf.at[h, l, pl.ds(0, 144)], rh.at[0, dl], gs.at[8 + 4 * e], gr.at[8 + 4 * e], heavy(1))
        go(gbuf.at[h, l, pl.ds(144, 144)], rh.at[1, dl], gs.at[9 + 4 * e], gr.at[9 + 4 * e], heavy(3))

    @pl.when(jnp.logical_not(early))
    def _():
        ours()
        send_ours()

    for e in range(4):
        dl = lorder[e]
        for k, dh in ((0, 1), (1, 3)):
            h, l = grad(dh, dl)
            part = pl.ds(k * 144, 144)
            n = 8 + 4 * e + k
            got(rh.at[k, dl], gs.at[n], gr.at[n])
            gbuf[h, l, part] = (gbuf[h, l, part].astype(F32) + rh[k, dl].astype(F32)).astype(BF16)
            go(gbuf.at[h, l], r1.at[k, dl], gs.at[n + 2], gr.at[n + 2], heavy(dh))
    for e in range(4):
        dl = lorder[e]
        h, l = grad(0, dl)
        total = gbuf[h, l].astype(F32)
        for k in range(2):
            n = 10 + 4 * e + k
            got(r1.at[k, dl], gs.at[n], gr.at[n])
            total += r1[k, dl].astype(F32)
        if dl:
            s2[dl - 1] = total.astype(BF16)
            go(s2.at[dl - 1], r2.at[dl - 1], gs.at[23 + dl], gr.at[23 + dl], light(dl))
        else:
            fin[...] = total
    for dl in (2, 1, 3):
        got(r2.at[dl - 1], gs.at[23 + dl], gr.at[23 + dl])
        fin[...] += r2[dl - 1].astype(F32)

    def rows_for(zl_, c_):
        even = c_ == 0
        lo = jnp.where(even, fin[192:214], fin[214:236])
        hi_ = jnp.where(even, fin[236:258], fin[258:280])
        return fin[pl.ds(pl.multiple_of(zl_ * 96 + c_ * 48, 48), 48)], jnp.where(zl_ == 0, lo, hi_)

    dests = ((1 - zl, 1 - c), (1 - zl, c), (zl, 1 - c))
    for k in range(3):
        a, b = rows_for(*dests[k])
        cs[k, 0:48] = a.astype(BF16)
        cs[k, 48:80] = jnp.concatenate([b, jnp.zeros((10, 512), F32)], axis=0).astype(BF16)
        go(cs.at[k], cr.at[k], gs.at[27 + k], gr.at[27 + k], dev(x, y, dests[k][0], dests[k][1], t))
    factor = 1.0 / 128.0
    mine = pl.ds(pl.multiple_of(c * 512, 512), 512)
    other = pl.ds(pl.multiple_of((1 - c) * 512, 512), 512)
    a, b = rows_for(zl, c)
    for k in range(3):
        got(cr.at[k], gs.at[27 + k], gr.at[27 + k])
    in_out[:, mine] = (a + cr[1, 0:48].astype(F32)) * factor
    out_out[:, mine] = (b + cr[1, 48:80].astype(F32)[0:22]) * factor
    in_out[:, other] = (cr[0, 0:48].astype(F32) + cr[2, 0:48].astype(F32)) * factor
    out_out[:, other] = (cr[0, 48:80].astype(F32) + cr[2, 48:80].astype(F32))[0:22] * factor

    for j in range(4):
        to_pair(j).wait_recv()
        to_pair(j).wait_send()
        to_sib(j).wait_send()
        keep(j).wait()
    for g in both:
        g.end0()
    for cp in sent:
        cp.wait_send()


def close_kernel(a, b, in_ref, out_ref, state, in_grad, out_grad):
    state[...] = a[...].astype(F32) + b[...].astype(F32)

    @pl.when(pl.program_id(0) == 0)
    def _():
        in_grad[...] = in_ref[...]
        out_grad[...] = out_ref[...]


def close(a, b, in_grad, out_grad):
    rows = pl.BlockSpec((128, HID), lambda i: (i, 0))
    whole = [pl.BlockSpec(v.shape, lambda i: (0, 0)) for v in (in_grad, out_grad)]
    return pl.pallas_call(
        close_kernel,
        grid=(2,),
        out_shape=(
            jax.ShapeDtypeStruct((256, HID), F32),
            jax.ShapeDtypeStruct(in_grad.shape, F32),
            jax.ShapeDtypeStruct(out_grad.shape, F32),
        ),
        in_specs=[rows, rows] + whole,
        out_specs=(rows, *whole),
        name="close",
    )(a, b, in_grad, out_grad)


def on_device(
    enc_input, norm_gain, fc_in, fc_out, final_gain, hidden_states, timestep, patch_order, proj_in, proj_out
):
    vm = pl.BlockSpec(memory_space=pltpu.VMEM)
    anyspace = pl.BlockSpec(memory_space=pl.ANY)
    V = pltpu.VMEM
    D = pltpu.SemaphoreType.DMA
    scratch = [
        V((96, 1024), BF16), V((SLOTS_FC, ENC, CH), BF16), V((SLOTS_FC, CH, ENC), BF16),
        V((2, 128, ENC), F32), V((256, ENC), BF16), V((2, 128, ENC), F32),
        V((128, ENC), BF16), V((128, ENC), BF16), V((8, 16, ENC), BF16), V((8, 16, ENC), BF16),
        V((4, 2, 4, 96, 512), BF16), V((4, 2, 4, 48, 512), BF16), V((ENC, 512), BF16),
        V((2, 256, HID), BF16), V((HID, 512), BF16),
        V((2, 2, 128, 512), F32), V((2, 2, 128, 512), BF16),
        V((2, 128, ENC), BF16), V((2, 128, ENC), BF16), V((2, 128, ENC), F32),
        V((128, ENC), BF16), V((128, ENC), BF16), V((2, 2, 128, ENC), BF16), V((ENC, 512), BF16),
        V((2, 2, 128, 512), BF16),
        V((1416, 512), F32), V((4, 4, 288, 512), BF16), V((2, 4, 144, 512), BF16), V((2, 4, 288, 512), BF16),
        V((3, 288, 512), BF16), V((3, 288, 512), BF16), V((288, 512), F32),
        V((3, 80, 512), BF16), V((3, 80, 512), BF16),
        V((4, 256, 768), BF16), V((4, 256, 768), BF16), V((4, 256, 768), BF16),
        D((2, NCH)), D((7,)), D((26,)), D((26,)), D((26,)), D((26,)),
        D((18,)), D((18,)), D((8,)), D((8,)), D((30,)), D((30,)), D((2,)), D((2,)),
    ]
    zs, zr, in_grad, out_grad = pl.pallas_call(
        kernel,
        out_shape=(
            jax.ShapeDtypeStruct((256, HID), BF16),
            jax.ShapeDtypeStruct((256, HID), BF16),
            jax.ShapeDtypeStruct((48, 1024), F32),
            jax.ShapeDtypeStruct((22, 1024), F32),
        ),
        in_specs=[vm] * 4 + [pl.BlockSpec(memory_space=pltpu.SMEM)] + [vm] * 2 + [anyspace] * 3,
        out_specs=(anyspace, anyspace, vm, vm),
        scratch_shapes=scratch,
        compiler_params=pltpu.CompilerParams(
            collective_id=0, has_side_effects=True, vmem_limit_bytes=62 << 20
        ),
        name="fused",
    )(
        enc_input, patch_order, norm_gain, final_gain, timestep,
        proj_in, proj_out, hidden_states, fc_in, fc_out,
    )
    return close(zs, zr, in_grad, out_grad)


def solution(mesh):
    in_specs = (
        P(("dp", "seq"), None),
        P(),
        P(None, "tensor"),
        P("tensor", None),
        P(),
        P(("dp", "seq"), None),
        P("dp"),
        P(),
        P("seq", "tensor"),
        P("seq", "tensor"),
    )
    out_specs = (P(("dp", "seq"), None), P(("dp", "seq"), "tensor"), P(("dp", "seq"), "tensor"))
    return jax.shard_map(
        on_device, mesh=mesh, in_specs=in_specs, out_specs=out_specs, check_vma=False
    )
```
